32 devices in a mesh: ctx: 16 (over z, x, core), head: 2 (over y).
Axes of the slice: x: 2, y: 2, z: 4, core: 2. Of those that a mesh axis runs over, the one named last changes fastest.
Arguments:
- queries: bfloat16 [4096, 3584], P(('ctx', 'head')), may hold values from -40 to 40
- local_key_value: bfloat16 [4096, 1024], P(('ctx', 'head')), may hold values from -40 to 40
- cached_key_value: bfloat16 [16384, 1024], P('ctx'), may hold values from -40 to 40
- vert_index: int32 [28, 12], replicated, may hold values from 0 to 255, as said below
- vert_count: int32 [28], replicated, may hold values from 3 to 12
- slash_off: int32 [28, 4], replicated, may hold values from 0 to 3, as said below
- slash_count: int32 [28], replicated, may hold values from 1 to 4
- head_owner: int32 [28], replicated, may hold values from 0 to 1, as said below
Outputs:
- owned_heads: bfloat16 [2, 16, 4096, 128], P('head', None, 'ctx')
The draws below stay inside these ranges and needn't reach their ends.
Inputs may be any that keep to these rules, and one draw needn't show every extreme that they name: `vert_index`: the entries of a row are distinct. No more than 2 entries of one row lie in the run of 16 blocks held by one index of ctx, and in every row some index of ctx holds exactly 2 of its used entries. slash_off[h, 0] = 0 for every head, and the entries of a row are distinct. `head_owner`: every index of head owns at least one query head and at most 16; some owner holds exactly 16.
All inputs are finite; a program needn't handle non-finite values.
Results may differ from the reference program's by a relative error of at most 0.005.
Values may be sent and summed in bfloat16 or wider, within the bound.
A program may use at most 128 MiB of HBM per device.

```python
import math
import jax
import jax.numpy as jnp
from jax import lax

QUERY_HEADS = 28
KEY_VALUE_HEADS = 4
HEAD_SIZE = 128
BLOCK_TOKENS = 64
SPAN = 4
SLASH = 4
VERTICAL_LIMIT = 2
Q_CTX = 256
CACHE_DEV = 1024
QUERY_LENGTH = 4096
CACHE_TOKENS = 16384
VTOT = 12
HCAP = 16
N_HEAD = 2


def draw_queries(key, part):
    key = jax.random.fold_in(key, 5)
    key_start_offset = jax.random.fold_in(key, 0)
    value_rows = jax.random.normal(key_start_offset, (QUERY_LENGTH, QUERY_HEADS, HEAD_SIZE), jnp.float32)
    return jnp.clip(value_rows, -40.0, 40.0).reshape(QUERY_LENGTH, QUERY_HEADS * HEAD_SIZE).astype(jnp.bfloat16)


def draw_cached_key_value(key, part):
    key = jax.random.fold_in(key, 7)
    key_start_offset = jax.random.fold_in(key, 0)
    value_rows = jax.random.normal(key_start_offset, (CACHE_TOKENS, KEY_VALUE_HEADS, 2, HEAD_SIZE), jnp.float32)
    return jnp.clip(value_rows, -40.0, 40.0).reshape(CACHE_TOKENS, KEY_VALUE_HEADS * 2 * HEAD_SIZE).astype(jnp.bfloat16)


def draw_local_key_value(key, part):
    key = jax.random.fold_in(key, 9)
    key_start_offset = jax.random.fold_in(key, 0)
    value_rows = jax.random.normal(key_start_offset, (QUERY_LENGTH, KEY_VALUE_HEADS, 2, HEAD_SIZE), jnp.float32)
    return jnp.clip(value_rows, -40.0, 40.0).reshape(QUERY_LENGTH, KEY_VALUE_HEADS * 2 * HEAD_SIZE).astype(jnp.bfloat16)


def draw_vert_index(key, part):
    key = jax.random.fold_in(key, 11)
    key_start_offset, key_hot = jax.random.split(key)
    partition_count = CACHE_TOKENS // CACHE_DEV
    per_shard = CACHE_DEV // BLOCK_TOKENS
    overall_block_count = CACHE_TOKENS // BLOCK_TOKENS
    block_numbers = jnp.arange(overall_block_count)
    partition_owner = block_numbers // per_shard
    start_offset = jax.random.randint(key_start_offset, (QUERY_HEADS, overall_block_count), 0, 1000)
    hot_keys = jax.random.split(key_hot, QUERY_HEADS)
    hot_order = jax.vmap(lambda row_key: jax.random.permutation(row_key, partition_count))(hot_keys)
    hot_rank = jnp.sum(jnp.where(hot_order[:, :, None] == jnp.arange(partition_count)[None, None, :], jnp.arange(partition_count)[None, :, None], 0), axis=1)
    busiest_partition = hot_rank < 3
    extra_score = jnp.where(busiest_partition[:, partition_owner], 3000, 0)
    extra_score = extra_score + jnp.where(partition_owner == partition_count - 1, 5000, 0)[None, :]
    extra_score = extra_score + jnp.where(block_numbers < VERTICAL_LIMIT, 10000, 0)[None, :]
    attention_scores = (start_offset + extra_score) * overall_block_count + block_numbers[None, :]
    grouped = attention_scores.reshape(QUERY_HEADS, partition_count, per_shard)
    above = jnp.sum((grouped[:, :, None, :] > grouped[:, :, :, None]).astype(jnp.int32), axis=3)
    eligible = (above < VERTICAL_LIMIT).reshape(QUERY_HEADS, overall_block_count)
    attention_scores = jnp.where(eligible, attention_scores, -1 - block_numbers[None, :])
    chosen_scores, chosen_blocks = lax.top_k(attention_scores, VTOT)
    return chosen_blocks.astype(jnp.int32)


def draw_slash_off(key, part):
    key = jax.random.fold_in(key, 17)
    row_keys = jax.random.split(key, QUERY_HEADS)

    def one_row(row_key):
        further = jax.random.permutation(row_key, SPAN - 1)[:SLASH - 1] + 1
        return jnp.concatenate([jnp.zeros((1,), jnp.int32), further.astype(jnp.int32)])
    return jax.vmap(one_row)(row_keys)


def draw_head_owner(key, part):
    key = jax.random.fold_in(key, 13)
    key_labels, key_heads = jax.random.split(key)
    remaining = QUERY_HEADS - HCAP
    common = remaining // (N_HEAD - 1)
    leftover = remaining % (N_HEAD - 1)
    owner_ids = jnp.arange(N_HEAD)
    counts = jnp.where(owner_ids == 0, HCAP, common + (owner_ids - 1 < leftover).astype(jnp.int32))
    boundary = jnp.cumsum(counts)
    positions = jnp.arange(QUERY_HEADS)
    labels = jnp.sum((boundary[None, :] <= positions[:, None]).astype(jnp.int32), axis=1)
    relabel = jax.random.permutation(key_labels, N_HEAD)
    shuffle = jax.random.permutation(key_heads, QUERY_HEADS)
    return relabel[labels][shuffle].astype(jnp.int32)


def set_ends(result, rng, least, high):
    extent = result.shape
    index_at = [jax.random.randint(jax.random.fold_in(rng, axis), (), 0, extent[axis]) for axis in range(len(extent))]
    result = result.at[tuple(index_at)].set(least)
    longest = extent.index(max(extent))
    index_at[longest] = (index_at[longest] + 1) % extent[longest]
    return result.at[tuple(index_at)].set(high)


def setup_inputs(seed: int = 0) -> dict:
    keys = jax.random.split(jax.random.key(seed), 9)
    return {
        "queries": draw_queries(jax.random.fold_in(keys[8], 71), 0),
        "local_key_value": draw_local_key_value(jax.random.fold_in(keys[8], 71), 0),
        "cached_key_value": draw_cached_key_value(jax.random.fold_in(keys[8], 71), 0),
        "vert_index": draw_vert_index(jax.random.fold_in(keys[8], 71), 0),
        "vert_count": set_ends(jax.random.randint(keys[4], (QUERY_HEADS,), max(VTOT // 4, VERTICAL_LIMIT), VTOT + 1), jax.random.fold_in(keys[4], 1), max(VTOT // 4, VERTICAL_LIMIT), VTOT).astype(jnp.int32),
        "slash_off": draw_slash_off(jax.random.fold_in(keys[8], 71), 0),
        "slash_count": set_ends(jax.random.randint(keys[6], (QUERY_HEADS,), 1, SLASH + 1), jax.random.fold_in(keys[6], 1), 1, SLASH).astype(jnp.int32),
        "head_owner": draw_head_owner(jax.random.fold_in(keys[8], 71), 0),
    }


masked_score = -1e+30

def slot_table(head_owner, owners, capacity):
    head_total = head_owner.shape[0]
    positions = jnp.arange(head_total)
    same_owner = head_owner[None, :] == head_owner[:, None]
    before = positions[None, :] < positions[:, None]
    ranking = lax.optimization_barrier(jnp.sum((same_owner & before).astype(jnp.int32), axis=1))
    owner_ids = jnp.arange(owners)
    slot_ids = jnp.arange(capacity)
    return (head_owner[None, None, :] == owner_ids[:, None, None]) & (ranking[None, None, :] == slot_ids[None, :, None])

def attend_block(query_rows, vertical_keys, vertical_values, vertical_live, slash_tiles, offsets, slash_live):
    score_scale = 1.0 / math.sqrt(HEAD_SIZE)
    row_count = query_rows.shape[0]
    blocks_here = row_count // BLOCK_TOKENS
    vertical_scores = jnp.dot(query_rows, vertical_keys.T, preferred_element_type=jnp.float32) * score_scale
    vertical_scores = jnp.where(vertical_live[None, :], vertical_scores, masked_score)
    slash_keys = slash_tiles[..., :HEAD_SIZE].astype(jnp.float32)
    slash_values = slash_tiles[..., HEAD_SIZE:].astype(jnp.float32).reshape(blocks_here, SLASH * BLOCK_TOKENS, HEAD_SIZE)
    grouped = query_rows.reshape(blocks_here, BLOCK_TOKENS, HEAD_SIZE).astype(jnp.float32)
    slash_scores = jnp.einsum('aid,akjd->aikj', grouped, slash_keys) * score_scale
    within = jnp.arange(BLOCK_TOKENS)
    causal = (offsets[None, None, :, None] > 0) | (within[None, :, None, None] >= within[None, None, None, :])
    allowed = slash_live[:, None, :, None] & causal
    slash_scores = jnp.where(allowed, slash_scores, masked_score).reshape(blocks_here, BLOCK_TOKENS, SLASH * BLOCK_TOKENS)
    highest = jnp.maximum(lax.optimization_barrier(jnp.max(vertical_scores, axis=1)).reshape(blocks_here, BLOCK_TOKENS), lax.optimization_barrier(jnp.max(slash_scores, axis=2)))
    vertical_weights = jnp.exp(vertical_scores - highest.reshape(row_count)[:, None])
    slash_weights = jnp.exp(slash_scores - highest[:, :, None])
    weight_sum = lax.optimization_barrier(jnp.sum(vertical_weights, axis=1)) + lax.optimization_barrier(jnp.sum(slash_weights, axis=2)).reshape(row_count)
    weighted = jnp.dot(vertical_weights.astype(jnp.bfloat16), vertical_values, preferred_element_type=jnp.float32)
    slash_rounded = lax.optimization_barrier(slash_weights.astype(jnp.bfloat16)).astype(jnp.float32)
    weighted = weighted + jnp.einsum('aim,amd->aid', slash_rounded, slash_values).reshape(row_count, HEAD_SIZE)
    return (weighted / weight_sum[:, None]).astype(jnp.bfloat16)

def reference(queries, local_key_value, cached_key_value, vert_index, vert_count, slash_off, slash_count, head_owner):
    overall_row_count = queries.shape[0]
    per_block = Q_CTX // BLOCK_TOKENS
    row_blocks = overall_row_count // Q_CTX
    cached_block_count = cached_key_value.reshape(CACHE_TOKENS // BLOCK_TOKENS, BLOCK_TOKENS, KEY_VALUE_HEADS, 2 * HEAD_SIZE)
    local_block_count = local_key_value.reshape(overall_row_count // BLOCK_TOKENS, BLOCK_TOKENS, KEY_VALUE_HEADS, 2 * HEAD_SIZE)
    query_group_width = QUERY_HEADS // KEY_VALUE_HEADS

    def one_head(head_id):
        kv_group = head_id // query_group_width
        listed = cached_block_count[vert_index[head_id], :, kv_group, :]
        vertical_keys = listed[..., :HEAD_SIZE].reshape(VTOT * BLOCK_TOKENS, HEAD_SIZE)
        vertical_values = listed[..., HEAD_SIZE:].reshape(VTOT * BLOCK_TOKENS, HEAD_SIZE)
        vertical_live = jnp.repeat(jnp.arange(VTOT) < vert_count[head_id], BLOCK_TOKENS)
        offsets = slash_off[head_id]
        slot_used = jnp.arange(SLASH) < slash_count[head_id]
        head_queries = lax.dynamic_slice_in_dim(queries, (head_id * HEAD_SIZE).astype(jnp.int32), HEAD_SIZE, 1)
        group_stretch = local_block_count[:, :, kv_group, :]

        def one_block(row_block):
            first_row = (row_block * Q_CTX).astype(jnp.int32)
            query_rows = lax.dynamic_slice_in_dim(head_queries, first_row, Q_CTX, 0)
            targets = row_block * per_block + jnp.arange(per_block)[:, None] - offsets[None, :]
            slash_live = (targets >= 0) & slot_used[None, :]
            slash_tiles = group_stretch[jnp.maximum(targets, 0)]
            return attend_block(query_rows, vertical_keys, vertical_values, vertical_live, slash_tiles, offsets, slash_live)
        return lax.map(one_block, jnp.arange(row_blocks, dtype=jnp.int32)).reshape(overall_row_count, HEAD_SIZE)
    attended = lax.map(one_head, jnp.arange(QUERY_HEADS, dtype=jnp.int32))
    slot_map = slot_table(head_owner, N_HEAD, HCAP)
    slot_heads = lax.optimization_barrier(jnp.sum(jnp.where(slot_map, jnp.arange(QUERY_HEADS)[None, None, :], 0), axis=2))
    slot_live = jnp.any(slot_map, axis=2)
    owned_rows = attended[slot_heads]
    return jnp.where(slot_live[:, :, None, None], owned_rows, jnp.zeros((), jnp.bfloat16))
```

```python
import functools
import math

import jax
import jax.numpy as jnp
from jax import lax
from jax.experimental import pallas as pl
from jax.experimental.pallas import tpu as pltpu
from jax.sharding import PartitionSpec as P

QUERY_HEADS = 28
KEY_VALUE_HEADS = 4
HEAD_SIZE = 128
BLOCK_TOKENS = 64
SPAN = 4
SLASH = 4
GROUP_WIDTH = QUERY_HEADS // KEY_VALUE_HEADS

masked_score = -1e30
INFO = 8


def pick_kernel(
    owners,
    total_blocks,
    shard_blocks,
    capacity,
    list_length,
    ids,
    vert_index,
    vert_count,
    slash_off,
    slash_count,
    head_owner,
    cache,
    picked,
    place,
    info,
    used,
    seen,
    slots_of,
    tiles_of,
    sem,
):
    me = ids[0]
    first = ids[1] * shard_blocks
    picked[...] = jnp.zeros_like(picked)
    unroll = 16
    table = owners * KEY_VALUE_HEADS * total_blocks

    @pl.loop(0, table // unroll)
    def _(i):
        for u in range(unroll):
            seen[i * unroll + u] = 0

    for o in range(owners):
        slots_of[o] = 0
        tiles_of[o] = 0
    for s in range(capacity + 1):
        for u in range(INFO):
            info[s * INFO + u] = 0
        for j in range(list_length):
            place[s * list_length + j] = 0

    def one_head(h, started):
        owner = head_owner[h]
        mine = owner == me
        rank = slots_of[owner]
        slots_of[owner] = rank + 1
        slot = jnp.where(mine, rank, capacity)
        group = h // GROUP_WIDTH
        count = vert_count[h]
        bits = 0
        for k in range(SLASH):
            bits = bits | jnp.where(k < slash_count[h], 1 << slash_off[h, k], 0)
        info[slot * INFO] = h
        info[slot * INFO + 1] = group
        info[slot * INFO + 2] = count
        info[slot * INFO + 3] = bits
        info[slot * INFO + 4] = 1
        base = (owner * KEY_VALUE_HEADS + group) * total_blocks

        def one_entry(j, carry):
            tiles, started = carry
            block = vert_index[h, j]
            old = seen[base + block]
            fresh = old == 0
            at = jnp.where(fresh, tiles, old - 1)
            seen[base + block] = at + 1
            place[slot * list_length + j] = at
            here = fresh & mine & (block >= first) & (block < first + shard_blocks)

            @pl.when(here)
            def _():
                row = pl.multiple_of((block - first) * BLOCK_TOKENS, BLOCK_TOKENS)
                column = pl.multiple_of(group * 2 * HEAD_SIZE, 2 * HEAD_SIZE)
                pltpu.make_async_copy(
                    cache.at[pl.ds(row, BLOCK_TOKENS), pl.ds(column, 2 * HEAD_SIZE)],
                    picked.at[at],
                    sem,
                ).start()

            return tiles + fresh.astype(jnp.int32), started + here.astype(jnp.int32)

        tiles, started = lax.fori_loop(0, count, one_entry, (tiles_of[owner], started))
        tiles_of[owner] = tiles
        return started

    started = lax.fori_loop(0, QUERY_HEADS, one_head, jnp.int32(0))
    most = tiles_of[0]
    for o in range(1, owners):
        most = jnp.maximum(most, tiles_of[o])
    used[0] = most

    @pl.loop(0, started)
    def _(i):
        pltpu.make_async_copy(
            cache.at[pl.ds(0, BLOCK_TOKENS), pl.ds(0, 2 * HEAD_SIZE)], picked.at[0], sem
        ).wait()


def attend_kernel(list_length, place, info, ids, q_ref, kv_ref, tiles_ref, out_ref, listed):
    s = pl.program_id(0)
    scale = 1.0 / math.sqrt(HEAD_SIZE)
    count = info[s * INFO + 2]
    bits = info[s * INFO + 3]
    live = info[s * INFO + 4]
    rows = q_ref.shape[0]
    blocks = rows // BLOCK_TOKENS
    window = SPAN * BLOCK_TOKENS
    first_block = ids[1] * blocks

    @pl.when(live == 0)
    def _():
        out_ref[...] = jnp.zeros_like(out_ref)

    @pl.when(live != 0)
    def _():
        for j in range(list_length):
            listed[j * BLOCK_TOKENS : (j + 1) * BLOCK_TOKENS, :] = tiles_ref[
                place[s * list_length + j]
            ]
        q = q_ref[...]
        contract = (((1,), (1,)), ((), ()))
        vertical = lax.dot_general(
            q, listed[:, :HEAD_SIZE], contract, preferred_element_type=jnp.float32
        )
        spot = lax.broadcasted_iota(jnp.int32, (1, list_length * BLOCK_TOKENS), 1)
        vertical = jnp.where(spot < count * BLOCK_TOKENS, vertical, masked_score)
        column = lax.broadcasted_iota(jnp.int32, (1, window), 1)
        within = lax.broadcasted_iota(jnp.int32, (BLOCK_TOKENS, window), 0)
        across = lax.broadcasted_iota(jnp.int32, (BLOCK_TOKENS, window), 1)
        causal = across <= within + (SPAN - 1) * BLOCK_TOKENS
        for b in range(blocks):
            part = slice(b * BLOCK_TOKENS, (b + 1) * BLOCK_TOKENS)
            near = slice(b * BLOCK_TOKENS, b * BLOCK_TOKENS + window)
            slash = lax.dot_general(
                q[part], kv_ref[near, :HEAD_SIZE], contract, preferred_element_type=jnp.float32
            )
            open_ = jnp.zeros((1, window), jnp.int32)
            for w in range(SPAN):
                d = SPAN - 1 - w
                ok = ((bits >> d) & 1) * (first_block + b >= d).astype(jnp.int32)
                open_ = jnp.where(column // BLOCK_TOKENS == w, ok, open_)
            slash = jnp.where((open_ > 0) & causal, slash, masked_score)
            far = vertical[part]
            highest = jnp.maximum(
                jnp.max(far, axis=1, keepdims=True), jnp.max(slash, axis=1, keepdims=True)
            )
            far = jnp.exp((far - highest) * scale)
            slash = jnp.exp((slash - highest) * scale)
            total = jnp.sum(far, axis=1, keepdims=True) + jnp.sum(slash, axis=1, keepdims=True)
            weighted = jnp.dot(
                far.astype(jnp.bfloat16), listed[:, HEAD_SIZE:], preferred_element_type=jnp.float32
            ) + jnp.dot(
                slash.astype(jnp.bfloat16),
                kv_ref[near, HEAD_SIZE:],
                preferred_element_type=jnp.float32,
            )
            out_ref[0, 0, part, :] = (weighted / total).astype(jnp.bfloat16)


def attend(place, info, ids, queries, extended, tiles, capacity, list_length):
    rows = queries.shape[0]
    return pl.pallas_call(
        functools.partial(attend_kernel, list_length),
        out_shape=jax.ShapeDtypeStruct((1, capacity, rows, HEAD_SIZE), jnp.bfloat16),
        grid_spec=pltpu.PrefetchScalarGridSpec(
            num_scalar_prefetch=3,
            grid=(capacity,),
            in_specs=[
                pl.BlockSpec((rows, HEAD_SIZE), lambda s, place, info, ids: (0, info[s * INFO])),
                pl.BlockSpec(
                    (extended.shape[0], 2 * HEAD_SIZE),
                    lambda s, place, info, ids: (0, info[s * INFO + 1]),
                ),
                pl.BlockSpec(memory_space=pltpu.VMEM),
            ],
            out_specs=pl.BlockSpec(
                (1, 1, rows, HEAD_SIZE), lambda s, place, info, ids: (0, s, 0, 0)
            ),
            scratch_shapes=[pltpu.VMEM((list_length * BLOCK_TOKENS, 2 * HEAD_SIZE), jnp.bfloat16)],
        ),
        compiler_params=pltpu.CompilerParams(vmem_limit_bytes=48 * 1024 * 1024),
        name="attend",
    )(place, info, ids, queries, extended, tiles)


def body(
    queries,
    local_key_value,
    cached_key_value,
    vert_index,
    vert_count,
    slash_off,
    slash_count,
    head_owner,
):
    owners = lax.axis_size("head")
    shards = lax.axis_size("ctx")
    ids = jnp.stack([lax.axis_index("head"), lax.axis_index("ctx")]).astype(jnp.int32)
    capacity = QUERY_HEADS // owners + 2
    list_length = vert_index.shape[1]
    shard_blocks = cached_key_value.shape[0] // BLOCK_TOKENS
    total_blocks = shard_blocks * shards
    most = capacity * list_length
    smem = pl.BlockSpec(memory_space=pltpu.SMEM)
    picked, place, info, used = pl.pallas_call(
        functools.partial(
            pick_kernel, owners, total_blocks, shard_blocks, capacity, list_length
        ),
        out_shape=(
            jax.ShapeDtypeStruct((most, BLOCK_TOKENS, 2 * HEAD_SIZE), jnp.bfloat16),
            jax.ShapeDtypeStruct(((capacity + 1) * list_length,), jnp.int32),
            jax.ShapeDtypeStruct(((capacity + 1) * INFO,), jnp.int32),
            jax.ShapeDtypeStruct((1,), jnp.int32),
        ),
        in_specs=[smem] * 6 + [pl.BlockSpec(memory_space=pl.ANY)],
        out_specs=(pl.BlockSpec(memory_space=pltpu.VMEM), smem, smem, smem),
        scratch_shapes=[
            pltpu.SMEM((owners * KEY_VALUE_HEADS * total_blocks,), jnp.int32),
            pltpu.SMEM((owners,), jnp.int32),
            pltpu.SMEM((owners,), jnp.int32),
            pltpu.SemaphoreType.DMA,
        ],
        compiler_params=pltpu.CompilerParams(vmem_limit_bytes=32 * 1024 * 1024),
        name="pick",
    )(ids, vert_index, vert_count, slash_off, slash_count, head_owner, cached_key_value)

    gathered = lax.all_gather(queries, "head", axis=0, tiled=True)
    near = lax.all_gather(local_key_value, "head", axis=0, tiled=True)
    reach = (SPAN - 1) * BLOCK_TOKENS
    route = [(i, i + 1) for i in range(shards - 1)]
    behind = lax.ppermute(near[near.shape[0] - reach :], "ctx", route)
    extended = jnp.concatenate([behind, near], axis=0)

    def with_tiles(size):
        def run():
            tiles = lax.psum(picked[:size], "ctx")
            return attend(place, info, ids, gathered, extended, tiles, capacity, list_length)

        return run

    sizes = sorted({most // 3, most // 2, most * 2 // 3, most})
    choice = sum((used[0] > size).astype(jnp.int32) for size in sizes[:-1])
    return lax.switch(choice, [with_tiles(size) for size in sizes])


def solution(mesh):
    in_specs = (
        P(("ctx", "head"), None),
        P(("ctx", "head"), None),
        P("ctx", None),
        P(),
        P(),
        P(),
        P(),
        P(),
    )
    out_specs = P("head", None, "ctx", None)
    return jax.shard_map(body, mesh=mesh, in_specs=in_specs, out_specs=out_specs, check_vma=False)
```

```python
import functools
import math

import jax
import jax.numpy as jnp
from jax import lax
from jax.experimental import pallas as pl
from jax.experimental.pallas import tpu as pltpu
from jax.sharding import PartitionSpec as P

QUERY_HEADS = 28
KEY_VALUE_HEADS = 4
HEAD_SIZE = 128
BLOCK_TOKENS = 64
SPAN = 4
SLASH = 4
GROUP_WIDTH = QUERY_HEADS // KEY_VALUE_HEADS

masked_score = -1e30
INFO = 8


def pick_kernel(
    owners,
    total_blocks,
    shard_blocks,
    capacity,
    list_length,
    ids,
    vert_index,
    vert_count,
    slash_off,
    slash_count,
    head_owner,
    cache,
    picked,
    place,
    info,
    used,
    seen,
    slots_of,
    tiles_of,
    sem,
):
    me = ids[0]
    first = ids[1] * shard_blocks
    picked[...] = jnp.zeros_like(picked)
    unroll = 16
    table = owners * KEY_VALUE_HEADS * total_blocks

    @pl.loop(0, table // unroll)
    def _(i):
        for u in range(unroll):
            seen[i * unroll + u] = 0

    for o in range(owners):
        slots_of[o] = 0
        tiles_of[o] = 0
    for s in range(capacity + 1):
        for u in range(INFO):
            info[s * INFO + u] = 0
        for j in range(list_length):
            place[s * list_length + j] = 0

    def one_head(h, started):
        owner = head_owner[h]
        mine = owner == me
        rank = slots_of[owner]
        slots_of[owner] = rank + 1
        slot = jnp.where(mine, rank, capacity)
        group = h // GROUP_WIDTH
        count = vert_count[h]
        bits = 0
        for k in range(SLASH):
            bits = bits | jnp.where(k < slash_count[h], 1 << slash_off[h, k], 0)
        info[slot * INFO] = h
        info[slot * INFO + 1] = group
        info[slot * INFO + 2] = count
        info[slot * INFO + 3] = bits
        info[slot * INFO + 4] = 1
        base = (owner * KEY_VALUE_HEADS + group) * total_blocks

        def one_entry(j, carry):
            tiles, started = carry
            block = vert_index[h, j]
            old = seen[base + block]
            fresh = old == 0
            at = jnp.where(fresh, tiles, old - 1)
            seen[base + block] = at + 1
            place[slot * list_length + j] = at
            here = fresh & mine & (block >= first) & (block < first + shard_blocks)

            @pl.when(here)
            def _():
                row = pl.multiple_of((block - first) * BLOCK_TOKENS, BLOCK_TOKENS)
                column = pl.multiple_of(group * 2 * HEAD_SIZE, 2 * HEAD_SIZE)
                pltpu.make_async_copy(
                    cache.at[pl.ds(row, BLOCK_TOKENS), pl.ds(column, 2 * HEAD_SIZE)],
                    picked.at[at],
                    sem,
                ).start()

            return tiles + fresh.astype(jnp.int32), started + here.astype(jnp.int32)

        tiles, started = lax.fori_loop(0, count, one_entry, (tiles_of[owner], started))
        tiles_of[owner] = tiles
        return started

    started = lax.fori_loop(0, QUERY_HEADS, one_head, jnp.int32(0))
    most = tiles_of[0]
    for o in range(1, owners):
        most = jnp.maximum(most, tiles_of[o])
    used[0] = most

    @pl.loop(0, started)
    def _(i):
        pltpu.make_async_copy(
            cache.at[pl.ds(0, BLOCK_TOKENS), pl.ds(0, 2 * HEAD_SIZE)], picked.at[0], sem
        ).wait()


def attend_kernel(list_length, place, info, ids, q_ref, kv_ref, tiles_ref, out_ref, listed):
    s = pl.program_id(0)
    scale = 1.0 / math.sqrt(HEAD_SIZE)
    count = info[s * INFO + 2]
    bits = info[s * INFO + 3]
    live = info[s * INFO + 4]
    rows = q_ref.shape[0]
    blocks = rows // BLOCK_TOKENS
    window = SPAN * BLOCK_TOKENS
    first_block = ids[1] * blocks

    @pl.when(live == 0)
    def _():
        out_ref[...] = jnp.zeros_like(out_ref)

    @pl.when(live != 0)
    def _():
        for j in range(list_length):
            listed[j * BLOCK_TOKENS : (j + 1) * BLOCK_TOKENS, :] = tiles_ref[
                place[s * list_length + j]
            ]
        q = q_ref[...]
        contract = (((1,), (1,)), ((), ()))
        vertical = lax.dot_general(
            q, listed[:, :HEAD_SIZE], contract, preferred_element_type=jnp.float32
        )
        spot = lax.broadcasted_iota(jnp.int32, (1, list_length * BLOCK_TOKENS), 1)
        vertical = jnp.where(spot < count * BLOCK_TOKENS, vertical, masked_score)
        column = lax.broadcasted_iota(jnp.int32, (1, window), 1)
        within = lax.broadcasted_iota(jnp.int32, (BLOCK_TOKENS, window), 0)
        across = lax.broadcasted_iota(jnp.int32, (BLOCK_TOKENS, window), 1)
        causal = across <= within + (SPAN - 1) * BLOCK_TOKENS
        for b in range(blocks):
            part = slice(b * BLOCK_TOKENS, (b + 1) * BLOCK_TOKENS)
            near = slice(b * BLOCK_TOKENS, b * BLOCK_TOKENS + window)
            slash = lax.dot_general(
                q[part], kv_ref[near, :HEAD_SIZE], contract, preferred_element_type=jnp.float32
            )
            open_ = jnp.zeros((1, window), jnp.int32)
            for w in range(SPAN):
                d = SPAN - 1 - w
                ok = ((bits >> d) & 1) * (first_block + b >= d).astype(jnp.int32)
                open_ = jnp.where(column // BLOCK_TOKENS == w, ok, open_)
            slash = jnp.where((open_ > 0) & causal, slash, masked_score)
            far = vertical[part]
            highest = jnp.maximum(
                jnp.max(far, axis=1, keepdims=True), jnp.max(slash, axis=1, keepdims=True)
            )
            far = jnp.exp((far - highest) * scale)
            slash = jnp.exp((slash - highest) * scale)
            total = jnp.sum(far, axis=1, keepdims=True) + jnp.sum(slash, axis=1, keepdims=True)
            weighted = jnp.dot(
                far.astype(jnp.bfloat16), listed[:, HEAD_SIZE:], preferred_element_type=jnp.float32
            ) + jnp.dot(
                slash.astype(jnp.bfloat16),
                kv_ref[near, HEAD_SIZE:],
                preferred_element_type=jnp.float32,
            )
            out_ref[0, 0, part, :] = (weighted / total).astype(jnp.bfloat16)


def attend(place, info, ids, queries, extended, tiles, capacity, list_length):
    rows = queries.shape[0]
    return pl.pallas_call(
        functools.partial(attend_kernel, list_length),
        out_shape=jax.ShapeDtypeStruct((1, capacity, rows, HEAD_SIZE), jnp.bfloat16),
        grid_spec=pltpu.PrefetchScalarGridSpec(
            num_scalar_prefetch=3,
            grid=(capacity,),
            in_specs=[
                pl.BlockSpec((rows, HEAD_SIZE), lambda s, place, info, ids: (0, info[s * INFO])),
                pl.BlockSpec(
                    (extended.shape[0], 2 * HEAD_SIZE),
                    lambda s, place, info, ids: (0, info[s * INFO + 1]),
                ),
                pl.BlockSpec(memory_space=pltpu.VMEM),
            ],
            out_specs=pl.BlockSpec(
                (1, 1, rows, HEAD_SIZE), lambda s, place, info, ids: (0, s, 0, 0)
            ),
            scratch_shapes=[pltpu.VMEM((list_length * BLOCK_TOKENS, 2 * HEAD_SIZE), jnp.bfloat16)],
        ),
        compiler_params=pltpu.CompilerParams(vmem_limit_bytes=48 * 1024 * 1024),
        name="attend",
    )(place, info, ids, queries, extended, tiles)


CHUNK_TILES = 4
MESH = pl.DeviceIdType.MESH


def share_kernel(
    size,
    chunk,
    picked,
    queries,
    local_kv,
    tiles,
    all_queries,
    extended,
    own,
    core_in,
    right_in,
    left_in,
    right_out,
    left_out,
    final,
    cross_in,
    done,
    zeros,
    core_sems,
    right_sems,
    left_sems,
    cross_sems,
    out_sems,
    local_sems,
    write_sems,
    query_sems,
    near_sems,
    behind_send,
    behind_recv,
):
    ctx = lax.axis_index("ctx")
    head = lax.axis_index("head")
    shards = lax.axis_size("ctx")
    core = ctx % 2
    x = (ctx // 2) % 2
    z = ctx // 4
    planes = shards // 4
    half = size // 2
    chunks = half // chunk
    other_core = (ctx + 1 - 2 * core, head)
    other_x = (ctx + 2 - 4 * x, head)
    up = (ctx + 4, head)
    down = (ctx - 4, head)
    other_head = (ctx, 1 - head)
    rows = queries.shape[0]
    reach = (SPAN - 1) * BLOCK_TOKENS
    has_up = z < planes - 1
    has_down = z > 0
    has_next = ctx < shards - 1
    has_previous = ctx > 0

    barrier = pltpu.get_barrier_semaphore()

    def greet(device):
        pl.semaphore_signal(barrier, inc=1, device_id=device, device_id_type=MESH)

    greet(other_core)
    greet(other_x)
    greet(other_head)

    @pl.when(has_up)
    def _():
        greet(up)

    @pl.when(has_down)
    def _():
        greet(down)

    @pl.when(has_next)
    def _():
        greet((ctx + 1, head))
        greet((ctx + 1, 1 - head))

    @pl.when(has_previous)
    def _():
        greet((ctx - 1, head))
        greet((ctx - 1, 1 - head))

    peers = 3 + jnp.where(has_up, 1, 0) + jnp.where(has_down, 1, 0)
    peers = peers + jnp.where(has_next, 2, 0) + jnp.where(has_previous, 2, 0)
    pl.semaphore_wait(barrier, peers)

    def remote(src, dst, send, recv, device):
        return pltpu.make_async_remote_copy(
            src_ref=src,
            dst_ref=dst,
            send_sem=send,
            recv_sem=recv,
            device_id=device,
            device_id_type=MESH,
        )

    def piece(base, k):
        return pl.ds(base + k * chunk, chunk)

    def own_copy(k):
        return pltpu.make_async_copy(
            picked.at[piece(core * half, k)], own.at[piece(0, k)], local_sems.at[k]
        )

    def core_copy(k):
        return remote(
            picked.at[piece((1 - core) * half, k)],
            core_in.at[piece(0, k)],
            core_sems.at[0, k],
            core_sems.at[1, k],
            other_core,
        )

    def right_copy(k):
        return remote(
            right_out.at[piece(0, k)],
            right_in.at[piece(0, k)],
            right_sems.at[0, k],
            right_sems.at[1, k],
            up,
        )

    def left_copy(k):
        return remote(
            left_out.at[piece(0, k)],
            left_in.at[piece(0, k)],
            left_sems.at[0, k],
            left_sems.at[1, k],
            down,
        )

    def cross_copy(k):
        return remote(
            final.at[piece(0, k)],
            cross_in.at[piece(0, k)],
            cross_sems.at[0, k],
            cross_sems.at[1, k],
            other_x,
        )

    def out_copy(k, base):
        return remote(
            done.at[piece(0, k)],
            tiles.at[piece(base, k)],
            out_sems.at[0, k],
            out_sems.at[1, k],
            other_core,
        )

    def write_copy(k):
        return pltpu.make_async_copy(
            done.at[piece(0, k)], tiles.at[piece(core * half, k)], write_sems.at[k]
        )

    @pl.loop(0, chunks)
    def _(k):
        own_copy(k).start()
        core_copy(k).start()

    mine = pl.ds(pl.multiple_of(head * rows, rows), rows)
    near = pl.ds(pl.multiple_of(reach + head * rows, BLOCK_TOKENS), rows)
    near_copy = remote(
        local_kv, extended.at[near], near_sems.at[0], near_sems.at[1], other_head
    )
    query_copy = remote(
        queries, all_queries.at[mine], query_sems.at[0], query_sems.at[1], other_head
    )
    near_here = pltpu.make_async_copy(local_kv, extended.at[near], near_sems.at[2])
    query_here = pltpu.make_async_copy(queries, all_queries.at[mine], query_sems.at[2])
    first = reach - rows

    def behind_copy(which, target):
        if which == 0:
            src, dst = local_kv.at[rows - first :], extended.at[:first]
        else:
            src, dst = local_kv, extended.at[first:reach]
        device = (ctx + 1, head if target == 0 else 1 - head)
        return remote(src, dst, behind_send.at[target], behind_recv.at[which], device)

    zero_copy = pltpu.make_async_copy(zeros, extended.at[:reach], behind_recv.at[2])
    for which in range(2):

        @pl.when(has_next & (head == which))
        def _():
            behind_copy(which, 0).start()
            behind_copy(which, 1).start()

    near_copy.start()
    query_copy.start()
    near_here.start()
    query_here.start()

    @pl.when(jnp.logical_not(has_previous))
    def _():
        zeros[...] = jnp.zeros_like(zeros)
        zero_copy.start()

    @pl.when(jnp.logical_not(has_down))
    def _():
        right_in[...] = jnp.zeros_like(right_in)

    @pl.when(jnp.logical_not(has_up))
    def _():
        left_in[...] = jnp.zeros_like(left_in)

    late = jnp.maximum(z, planes - 1 - z)

    @pl.loop(0, chunks + planes + 1)
    def _(t):
        @pl.when(t < chunks)
        def _():
            own_copy(t).wait()
            core_copy(t).wait_recv()
            at = piece(0, t)
            own[at] = own[at] + core_in[at]

        k_right = t - z

        @pl.when((k_right >= 0) & (k_right < chunks))
        def _():
            @pl.when(has_down)
            def _():
                right_copy(k_right).wait_recv()

            at = piece(0, k_right)
            right_out[at] = own[at] + right_in[at]

            @pl.when(has_up)
            def _():
                right_copy(k_right).start()

        k_left = t - (planes - 1 - z)

        @pl.when((k_left >= 0) & (k_left < chunks))
        def _():
            @pl.when(has_up)
            def _():
                left_copy(k_left).wait_recv()

            at = piece(0, k_left)
            left_out[at] = own[at] + left_in[at]

            @pl.when(has_down)
            def _():
                left_copy(k_left).start()

        k_cross = t - late

        @pl.when((k_cross >= 0) & (k_cross < chunks))
        def _():
            at = piece(0, k_cross)
            final[at] = right_out[at] + left_in[at]
            cross_copy(k_cross).start()

        k_done = k_cross - 1

        @pl.when((k_done >= 0) & (k_done < chunks))
        def _():
            cross_copy(k_done).wait_recv()
            at = piece(0, k_done)
            done[at] = final[at] + cross_in[at]
            out_copy(k_done, core * half).start()
            write_copy(k_done).start()

    @pl.loop(0, chunks)
    def _(k):
        core_copy(k).wait_send()

        @pl.when(has_up)
        def _():
            right_copy(k).wait_send()

        @pl.when(has_down)
        def _():
            left_copy(k).wait_send()

        cross_copy(k).wait_send()
        out_copy(k, core * half).wait_send()
        out_copy(k, (1 - core) * half).wait_recv()
        write_copy(k).wait()

    near_copy.wait()
    query_copy.wait()
    near_here.wait()
    query_here.wait()
    for which in range(2):

        @pl.when(has_next & (head == which))
        def _():
            behind_copy(which, 0).wait_send()
            behind_copy(which, 1).wait_send()

        @pl.when(has_previous)
        def _():
            behind_copy(which, 0).wait_recv()

    @pl.when(jnp.logical_not(has_previous))
    def _():
        zero_copy.wait()


def share(picked, queries, local_key_value, size, number):
    chunk = CHUNK_TILES * (2 if size > 128 else 1)
    half = size // 2
    chunks = half // chunk
    rows, width = queries.shape
    reach = (SPAN - 1) * BLOCK_TOKENS
    kv_width = local_key_value.shape[1]
    tile = (BLOCK_TOKENS, 2 * HEAD_SIZE)
    hbm = pl.BlockSpec(memory_space=pl.ANY)
    pairs = pltpu.SemaphoreType.DMA((2, chunks))
    return pl.pallas_call(
        functools.partial(share_kernel, size, chunk),
        out_shape=(
            jax.ShapeDtypeStruct((size,) + tile, jnp.bfloat16),
            jax.ShapeDtypeStruct((2 * rows, width), jnp.bfloat16),
            jax.ShapeDtypeStruct((reach + 2 * rows, kv_width), jnp.bfloat16),
        ),
        in_specs=[hbm] * 3,
        out_specs=(hbm,) * 3,
        scratch_shapes=[pltpu.VMEM((half,) + tile, jnp.bfloat16)] * 9
        + [pltpu.VMEM((reach, kv_width), jnp.bfloat16)]
        + [pairs] * 5
        + [pltpu.SemaphoreType.DMA((chunks,))] * 2
        + [pltpu.SemaphoreType.DMA((3,))] * 2
        + [pltpu.SemaphoreType.DMA((2,)), pltpu.SemaphoreType.DMA((3,))],
        compiler_params=pltpu.CompilerParams(
            collective_id=number, has_side_effects=True, vmem_limit_bytes=48 * 1024 * 1024
        ),
        name="share",
    )(picked, queries, local_key_value)


def body(
    queries,
    local_key_value,
    cached_key_value,
    vert_index,
    vert_count,
    slash_off,
    slash_count,
    head_owner,
):
    owners = lax.axis_size("head")
    shards = lax.axis_size("ctx")
    ids = jnp.stack([lax.axis_index("head"), lax.axis_index("ctx")]).astype(jnp.int32)
    capacity = QUERY_HEADS // owners + 2
    list_length = vert_index.shape[1]
    shard_blocks = cached_key_value.shape[0] // BLOCK_TOKENS
    total_blocks = shard_blocks * shards
    most = capacity * list_length
    smem = pl.BlockSpec(memory_space=pltpu.SMEM)
    picked, place, info, used = pl.pallas_call(
        functools.partial(
            pick_kernel, owners, total_blocks, shard_blocks, capacity, list_length
        ),
        out_shape=(
            jax.ShapeDtypeStruct((most, BLOCK_TOKENS, 2 * HEAD_SIZE), jnp.bfloat16),
            jax.ShapeDtypeStruct(((capacity + 1) * list_length,), jnp.int32),
            jax.ShapeDtypeStruct(((capacity + 1) * INFO,), jnp.int32),
            jax.ShapeDtypeStruct((1,), jnp.int32),
        ),
        in_specs=[smem] * 6 + [pl.BlockSpec(memory_space=pl.ANY)],
        out_specs=(pl.BlockSpec(memory_space=pltpu.VMEM), smem, smem, smem),
        scratch_shapes=[
            pltpu.SMEM((owners * KEY_VALUE_HEADS * total_blocks,), jnp.int32),
            pltpu.SMEM((owners,), jnp.int32),
            pltpu.SMEM((owners,), jnp.int32),
            pltpu.SemaphoreType.DMA,
        ],
        compiler_params=pltpu.CompilerParams(vmem_limit_bytes=32 * 1024 * 1024),
        name="pick",
    )(ids, vert_index, vert_count, slash_off, slash_count, head_owner, cached_key_value)

    own_plan = owners == 2 and shards == 16 and queries.shape[0] == 2 * BLOCK_TOKENS
    reach = (SPAN - 1) * BLOCK_TOKENS

    def with_tiles(number, size):
        def run():
            if own_plan:
                tiles, gathered, extended = share(
                    picked, queries, local_key_value, size, number
                )
            else:
                gathered = lax.all_gather(queries, "head", axis=0, tiled=True)
                near = lax.all_gather(local_key_value, "head", axis=0, tiled=True)
                route = [(i, i + 1) for i in range(shards - 1)]
                behind = lax.ppermute(near[near.shape[0] - reach :], "ctx", route)
                extended = jnp.concatenate([behind, near], axis=0)
                tiles = lax.psum(picked[:size], "ctx")
            return attend(place, info, ids, gathered, extended, tiles, capacity, list_length)

        return run

    sizes = sorted({most * 5 // 12, most * 13 // 24, most * 2 // 3, most})
    choice = sum((used[0] > size).astype(jnp.int32) for size in sizes[:-1])
    return lax.switch(choice, [with_tiles(i, size) for i, size in enumerate(sizes)])


def solution(mesh):
    in_specs = (
        P(("ctx", "head"), None),
        P(("ctx", "head"), None),
        P("ctx", None),
        P(),
        P(),
        P(),
        P(),
        P(),
    )
    out_specs = P("head", None, "ctx", None)
    return jax.shard_map(body, mesh=mesh, in_specs=in_specs, out_specs=out_specs, check_vma=False)
```

```python
import functools
import math

import jax
import jax.numpy as jnp
from jax import lax
from jax.experimental import pallas as pl
from jax.experimental.pallas import tpu as pltpu
from jax.sharding import PartitionSpec as P

QUERY_HEADS = 28
KEY_VALUE_HEADS = 4
HEAD_SIZE = 128
BLOCK_TOKENS = 64
SPAN = 4
SLASH = 4
GROUP_WIDTH = QUERY_HEADS // KEY_VALUE_HEADS

masked_score = -1e30
INFO = 8
LEAD = SPAN * BLOCK_TOKENS
PAIR = 2 * BLOCK_TOKENS


def pick_kernel(
    owners,
    total_blocks,
    shard_blocks,
    capacity,
    list_length,
    ids,
    vert_index,
    vert_count,
    slash_off,
    slash_count,
    head_owner,
    cache,
    picked,
    place,
    info,
    used,
    seen,
    slots_of,
    tiles_of,
    sem,
):
    me = ids[0]
    first = ids[1] * shard_blocks
    picked[...] = jnp.zeros_like(picked)
    unroll = 16
    table = owners * KEY_VALUE_HEADS * total_blocks

    @pl.loop(0, table // unroll)
    def _(i):
        for u in range(unroll):
            seen[i * unroll + u] = 0

    for o in range(owners):
        slots_of[o] = 0
        tiles_of[o] = 0
    for s in range(capacity + 1):
        for u in range(INFO):
            info[s * INFO + u] = 0
        for j in range(list_length):
            place[s * list_length + j] = 0

    def one_head(h, started):
        owner = head_owner[h]
        mine = owner == me
        rank = slots_of[owner]
        slots_of[owner] = rank + 1
        slot = jnp.where(mine, rank, capacity)
        group = h // GROUP_WIDTH
        count = vert_count[h]
        bits = 0
        for k in range(SLASH):
            bits = bits | jnp.where(k < slash_count[h], 1 << slash_off[h, k], 0)
        info[slot * INFO] = h
        info[slot * INFO + 1] = group
        info[slot * INFO + 2] = count
        info[slot * INFO + 3] = bits
        info[slot * INFO + 4] = 1
        base = (owner * KEY_VALUE_HEADS + group) * total_blocks

        def one_entry(j, carry):
            tiles, started = carry
            block = vert_index[h, j]
            old = seen[base + block]
            fresh = old == 0
            at = jnp.where(fresh, tiles, old - 1)
            seen[base + block] = at + 1
            place[slot * list_length + j] = at
            here = fresh & mine & (block >= first) & (block < first + shard_blocks)

            @pl.when(here)
            def _():
                row = pl.multiple_of((block - first) * BLOCK_TOKENS, BLOCK_TOKENS)
                column = pl.multiple_of(group * 2 * HEAD_SIZE, 2 * HEAD_SIZE)
                pltpu.make_async_copy(
                    cache.at[pl.ds(row, BLOCK_TOKENS), pl.ds(column, 2 * HEAD_SIZE)],
                    picked.at[at],
                    sem,
                ).start()

            return tiles + fresh.astype(jnp.int32), started + here.astype(jnp.int32)

        tiles, started = lax.fori_loop(0, count, one_entry, (tiles_of[owner], started))
        tiles_of[owner] = tiles
        return started

    started = lax.fori_loop(0, QUERY_HEADS, one_head, jnp.int32(0))
    most = tiles_of[0]
    for o in range(1, owners):
        most = jnp.maximum(most, tiles_of[o])
    used[0] = most

    @pl.loop(0, started)
    def _(i):
        pltpu.make_async_copy(
            cache.at[pl.ds(0, BLOCK_TOKENS), pl.ds(0, 2 * HEAD_SIZE)], picked.at[0], sem
        ).wait()


def attend_kernel(
    list_length, place, info, ids, q_ref, kv_ref, tiles_ref, out_ref, listed, offset_of
):
    s = pl.program_id(0)
    scale = 1.0 / math.sqrt(HEAD_SIZE)
    count = info[s * INFO + 2]
    bits = info[s * INFO + 3]
    live = info[s * INFO + 4]
    rows = q_ref.shape[0]
    pairs = rows // PAIR
    window = LEAD + PAIR
    unlisted = 31
    contract = (((1,), (1,)), ((), ()))

    @pl.when(s == 0)
    def _():
        row = lax.broadcasted_iota(jnp.int32, (PAIR, window), 0)
        column = lax.broadcasted_iota(jnp.int32, (PAIR, window), 1)
        offset = SPAN + row // BLOCK_TOKENS - column // BLOCK_TOKENS
        seen = (offset >= 0) & (offset < SPAN) & (column <= row + LEAD)
        for p in range(pairs):
            block = (ids[1] * rows + p * PAIR + row) // BLOCK_TOKENS
            offset_of[p] = jnp.where(seen & (block >= offset), offset, unlisted)

    @pl.when(live == 0)
    def _():
        out_ref[...] = jnp.zeros_like(out_ref)

    def attend_listed(length):
        for j in range(length):
            listed[j * BLOCK_TOKENS : (j + 1) * BLOCK_TOKENS, :] = tiles_ref[
                place[s * list_length + j]
            ]
        width = length * BLOCK_TOKENS
        far = lax.dot_general(
            q_ref[...], listed[:width, :HEAD_SIZE], contract, preferred_element_type=jnp.float32
        )
        spot = lax.broadcasted_iota(jnp.int32, (1, width), 1)
        far = jnp.where(spot < count * BLOCK_TOKENS, far, masked_score)
        near = []
        for p in range(pairs):
            scores = lax.dot_general(
                q_ref[p * PAIR : (p + 1) * PAIR, :],
                kv_ref[p * PAIR : p * PAIR + window, :HEAD_SIZE],
                contract,
                preferred_element_type=jnp.float32,
            )
            allowed = (lax.shift_right_logical(bits, offset_of[p]) & 1) != 0
            near.append(jnp.where(allowed, scores, masked_score))
        highest = jnp.maximum(
            jnp.max(far, axis=1, keepdims=True),
            jnp.concatenate([jnp.max(part, axis=1, keepdims=True) for part in near], axis=0),
        )
        far = jnp.exp((far - highest) * scale)
        total = jnp.sum(far, axis=1, keepdims=True)
        weighted = jnp.dot(
            far.astype(jnp.bfloat16),
            listed[:width, HEAD_SIZE:],
            preferred_element_type=jnp.float32,
        )
        for p in range(pairs):
            part = slice(p * PAIR, (p + 1) * PAIR)
            weights = jnp.exp((near[p] - highest[part]) * scale)
            share_sum = total[part] + jnp.sum(weights, axis=1, keepdims=True)
            share = weighted[part] + jnp.dot(
                weights.astype(jnp.bfloat16),
                kv_ref[p * PAIR : p * PAIR + window, HEAD_SIZE:],
                preferred_element_type=jnp.float32,
            )
            out_ref[0, 0, part, :] = (share / share_sum).astype(jnp.bfloat16)

    step = max(list_length // 3, 1)
    for length in range(step, list_length + 1, step):

        @pl.when((live != 0) & (count > length - step) & (count <= length))
        def _():
            attend_listed(length)


def attend(place, info, ids, queries, extended, tiles, capacity, list_length):
    rows = queries.shape[0]
    return pl.pallas_call(
        functools.partial(attend_kernel, list_length),
        out_shape=jax.ShapeDtypeStruct((1, capacity, rows, HEAD_SIZE), jnp.bfloat16),
        grid_spec=pltpu.PrefetchScalarGridSpec(
            num_scalar_prefetch=3,
            grid=(capacity,),
            in_specs=[
                pl.BlockSpec((rows, HEAD_SIZE), lambda s, place, info, ids: (0, info[s * INFO])),
                pl.BlockSpec(
                    (extended.shape[0], 2 * HEAD_SIZE),
                    lambda s, place, info, ids: (0, info[s * INFO + 1]),
                ),
                pl.BlockSpec(memory_space=pltpu.VMEM),
            ],
            out_specs=pl.BlockSpec(
                (1, 1, rows, HEAD_SIZE), lambda s, place, info, ids: (0, s, 0, 0)
            ),
            scratch_shapes=[
                pltpu.VMEM((list_length * BLOCK_TOKENS, 2 * HEAD_SIZE), jnp.bfloat16),
                pltpu.VMEM((rows // PAIR, PAIR, LEAD + PAIR), jnp.int32),
            ],
        ),
        compiler_params=pltpu.CompilerParams(vmem_limit_bytes=48 * 1024 * 1024),
        name="attend",
    )(place, info, ids, queries, extended, tiles)


CHUNK_TILES = 2
LAG = 3
MESH = pl.DeviceIdType.MESH


def share_kernel(
    size,
    chunk,
    picked,
    queries,
    local_kv,
    tiles,
    all_queries,
    extended,
    own,
    core_in,
    right_in,
    left_in,
    right_out,
    left_out,
    final,
    cross_in,
    done,
    zeros,
    core_sems,
    right_sems,
    left_sems,
    cross_sems,
    out_sems,
    local_sems,
    write_sems,
    query_sems,
    near_sems,
    behind_send,
    behind_recv,
):
    ctx = lax.axis_index("ctx")
    head = lax.axis_index("head")
    shards = lax.axis_size("ctx")
    core = ctx % 2
    x = (ctx // 2) % 2
    z = ctx // 4
    planes = shards // 4
    half = size // 2
    chunks = half // chunk
    other_core = (ctx + 1 - 2 * core, head)
    other_x = (ctx + 2 - 4 * x, head)
    up = (ctx + 4, head)
    down = (ctx - 4, head)
    other_head = (ctx, 1 - head)
    rows = queries.shape[0]
    has_up = z < planes - 1
    has_down = z > 0
    has_next = ctx < shards - 1
    has_previous = ctx > 0

    barrier = pltpu.get_barrier_semaphore()

    def greet(device):
        pl.semaphore_signal(barrier, inc=1, device_id=device, device_id_type=MESH)

    greet(other_core)
    greet(other_x)
    greet(other_head)

    @pl.when(has_up)
    def _():
        greet(up)

    @pl.when(has_down)
    def _():
        greet(down)

    @pl.when(has_next)
    def _():
        greet((ctx + 1, head))
        greet((ctx + 1, 1 - head))

    @pl.when(has_previous)
    def _():
        greet((ctx - 1, head))
        greet((ctx - 1, 1 - head))

    peers = 3 + jnp.where(has_up, 1, 0) + jnp.where(has_down, 1, 0)
    peers = peers + jnp.where(has_next, 2, 0) + jnp.where(has_previous, 2, 0)
    pl.semaphore_wait(barrier, peers)

    def remote(src, dst, send, recv, device):
        return pltpu.make_async_remote_copy(
            src_ref=src,
            dst_ref=dst,
            send_sem=send,
            recv_sem=recv,
            device_id=device,
            device_id_type=MESH,
        )

    def piece(base, k):
        return pl.ds(base + k * chunk, chunk)

    def own_copy(k):
        return pltpu.make_async_copy(
            picked.at[piece(core * half, k)], own.at[piece(0, k)], local_sems.at[k]
        )

    def core_copy(k):
        return remote(
            picked.at[piece((1 - core) * half, k)],
            core_in.at[piece(0, k)],
            core_sems.at[0, k],
            core_sems.at[1, k],
            other_core,
        )

    def right_copy(k):
        return remote(
            right_out.at[piece(0, k)],
            right_in.at[piece(0, k)],
            right_sems.at[0, k],
            right_sems.at[1, k],
            up,
        )

    def left_copy(k):
        return remote(
            left_out.at[piece(0, k)],
            left_in.at[piece(0, k)],
            left_sems.at[0, k],
            left_sems.at[1, k],
            down,
        )

    def cross_copy(k):
        return remote(
            final.at[piece(0, k)],
            cross_in.at[piece(0, k)],
            cross_sems.at[0, k],
            cross_sems.at[1, k],
            other_x,
        )

    def out_copy(k, base):
        return remote(
            done.at[piece(0, k)],
            tiles.at[piece(base, k)],
            out_sems.at[0, k],
            out_sems.at[1, k],
            other_core,
        )

    def write_copy(k):
        return pltpu.make_async_copy(
            done.at[piece(0, k)], tiles.at[piece(core * half, k)], write_sems.at[k]
        )

    @pl.loop(0, chunks)
    def _(k):
        own_copy(k).start()
        core_copy(k).start()

    mine = pl.ds(pl.multiple_of(head * rows, rows), rows)
    near = pl.ds(pl.multiple_of(LEAD + head * rows, BLOCK_TOKENS), rows)
    near_copy = remote(
        local_kv, extended.at[near], near_sems.at[0], near_sems.at[1], other_head
    )
    query_copy = remote(
        queries, all_queries.at[mine], query_sems.at[0], query_sems.at[1], other_head
    )
    near_here = pltpu.make_async_copy(local_kv, extended.at[near], near_sems.at[2])
    query_here = pltpu.make_async_copy(queries, all_queries.at[mine], query_sems.at[2])

    def behind_copy(which, target):
        src, dst = local_kv, extended.at[which * rows : (which + 1) * rows]
        device = (ctx + 1, head if target == 0 else 1 - head)
        return remote(src, dst, behind_send.at[target], behind_recv.at[which], device)

    zero_copy = pltpu.make_async_copy(zeros, extended.at[:LEAD], behind_recv.at[2])
    for which in range(2):

        @pl.when(has_next & (head == which))
        def _():
            behind_copy(which, 0).start()
            behind_copy(which, 1).start()

    near_copy.start()
    query_copy.start()
    near_here.start()
    query_here.start()

    @pl.when(jnp.logical_not(has_previous))
    def _():
        zeros[...] = jnp.zeros_like(zeros)
        zero_copy.start()

    @pl.when(jnp.logical_not(has_down))
    def _():
        right_in[...] = jnp.zeros_like(right_in)

    @pl.when(jnp.logical_not(has_up))
    def _():
        left_in[...] = jnp.zeros_like(left_in)

    late = LAG * jnp.maximum(z, planes - 1 - z)

    @pl.loop(0, chunks + LAG * planes)
    def _(t):
        @pl.when(t < chunks)
        def _():
            own_copy(t).wait()
            core_copy(t).wait_recv()
            at = piece(0, t)
            own[at] = own[at] + core_in[at]

        k_right = t - LAG * z

        @pl.when((k_right >= 0) & (k_right < chunks))
        def _():
            @pl.when(has_down)
            def _():
                right_copy(k_right).wait_recv()

            at = piece(0, k_right)
            right_out[at] = own[at] + right_in[at]

            @pl.when(has_up)
            def _():
                right_copy(k_right).start()

        k_left = t - LAG * (planes - 1 - z)

        @pl.when((k_left >= 0) & (k_left < chunks))
        def _():
            @pl.when(has_up)
            def _():
                left_copy(k_left).wait_recv()

            at = piece(0, k_left)
            left_out[at] = own[at] + left_in[at]

            @pl.when(has_down)
            def _():
                left_copy(k_left).start()

        k_cross = t - late

        @pl.when((k_cross >= 0) & (k_cross < chunks))
        def _():
            at = piece(0, k_cross)
            final[at] = right_out[at] + left_in[at]
            cross_copy(k_cross).start()

        k_done = k_cross - LAG

        @pl.when((k_done >= 0) & (k_done < chunks))
        def _():
            cross_copy(k_done).wait_recv()
            at = piece(0, k_done)
            done[at] = final[at] + cross_in[at]
            out_copy(k_done, core * half).start()
            write_copy(k_done).start()

    @pl.loop(0, chunks)
    def _(k):
        core_copy(k).wait_send()

        @pl.when(has_up)
        def _():
            right_copy(k).wait_send()

        @pl.when(has_down)
        def _():
            left_copy(k).wait_send()

        cross_copy(k).wait_send()
        out_copy(k, core * half).wait_send()
        out_copy(k, (1 - core) * half).wait_recv()
        write_copy(k).wait()

    near_copy.wait()
    query_copy.wait()
    near_here.wait()
    query_here.wait()
    for which in range(2):

        @pl.when(has_next & (head == which))
        def _():
            behind_copy(which, 0).wait_send()
            behind_copy(which, 1).wait_send()

        @pl.when(has_previous)
        def _():
            behind_copy(which, 0).wait_recv()

    @pl.when(jnp.logical_not(has_previous))
    def _():
        zero_copy.wait()


def share(picked, queries, local_key_value, size, number):
    chunk = CHUNK_TILES * (2 if size > 128 else 1)
    half = size // 2
    chunks = half // chunk
    rows, width = queries.shape
    kv_width = local_key_value.shape[1]
    tile = (BLOCK_TOKENS, 2 * HEAD_SIZE)
    hbm = pl.BlockSpec(memory_space=pl.ANY)
    pairs = pltpu.SemaphoreType.DMA((2, chunks))
    return pl.pallas_call(
        functools.partial(share_kernel, size, chunk),
        out_shape=(
            jax.ShapeDtypeStruct((size,) + tile, jnp.bfloat16),
            jax.ShapeDtypeStruct((2 * rows, width), jnp.bfloat16),
            jax.ShapeDtypeStruct((LEAD + 2 * rows, kv_width), jnp.bfloat16),
        ),
        in_specs=[hbm] * 3,
        out_specs=(hbm,) * 3,
        scratch_shapes=[pltpu.VMEM((half,) + tile, jnp.bfloat16)] * 9
        + [pltpu.VMEM((LEAD, kv_width), jnp.bfloat16)]
        + [pairs] * 5
        + [pltpu.SemaphoreType.DMA((chunks,))] * 2
        + [pltpu.SemaphoreType.DMA((3,))] * 2
        + [pltpu.SemaphoreType.DMA((2,)), pltpu.SemaphoreType.DMA((3,))],
        compiler_params=pltpu.CompilerParams(
            collective_id=number, has_side_effects=True, vmem_limit_bytes=48 * 1024 * 1024
        ),
        name="share",
    )(picked, queries, local_key_value)


def body(
    queries,
    local_key_value,
    cached_key_value,
    vert_index,
    vert_count,
    slash_off,
    slash_count,
    head_owner,
):
    owners = lax.axis_size("head")
    shards = lax.axis_size("ctx")
    ids = jnp.stack([lax.axis_index("head"), lax.axis_index("ctx")]).astype(jnp.int32)
    capacity = QUERY_HEADS // owners + 2
    list_length = vert_index.shape[1]
    shard_blocks = cached_key_value.shape[0] // BLOCK_TOKENS
    total_blocks = shard_blocks * shards
    most = capacity * list_length
    smem = pl.BlockSpec(memory_space=pltpu.SMEM)
    picked, place, info, used = pl.pallas_call(
        functools.partial(
            pick_kernel, owners, total_blocks, shard_blocks, capacity, list_length
        ),
        out_shape=(
            jax.ShapeDtypeStruct((most, BLOCK_TOKENS, 2 * HEAD_SIZE), jnp.bfloat16),
            jax.ShapeDtypeStruct(((capacity + 1) * list_length,), jnp.int32),
            jax.ShapeDtypeStruct(((capacity + 1) * INFO,), jnp.int32),
            jax.ShapeDtypeStruct((1,), jnp.int32),
        ),
        in_specs=[smem] * 6 + [pl.BlockSpec(memory_space=pl.ANY)],
        out_specs=(pl.BlockSpec(memory_space=pltpu.VMEM), smem, smem, smem),
        scratch_shapes=[
            pltpu.SMEM((owners * KEY_VALUE_HEADS * total_blocks,), jnp.int32),
            pltpu.SMEM((owners,), jnp.int32),
            pltpu.SMEM((owners,), jnp.int32),
            pltpu.SemaphoreType.DMA,
        ],
        compiler_params=pltpu.CompilerParams(vmem_limit_bytes=32 * 1024 * 1024),
        name="pick",
    )(ids, vert_index, vert_count, slash_off, slash_count, head_owner, cached_key_value)

    own_plan = owners == 2 and shards == 16 and queries.shape[0] == 2 * BLOCK_TOKENS

    def with_tiles(number, size):
        def run():
            if own_plan:
                tiles, gathered, extended = share(
                    picked, queries, local_key_value, size, number
                )
            else:
                gathered = lax.all_gather(queries, "head", axis=0, tiled=True)
                near = lax.all_gather(local_key_value, "head", axis=0, tiled=True)
                route = [(i, i + 1) for i in range(shards - 1)]
                behind = lax.ppermute(near[near.shape[0] - LEAD :], "ctx", route)
                extended = jnp.concatenate([behind, near], axis=0)
                tiles = lax.psum(picked[:size], "ctx")
            return attend(place, info, ids, gathered, extended, tiles, capacity, list_length)

        return run

    sizes = [most * part // 24 for part in (9, 10, 11, 12, 14, 24)]
    choice = sum((used[0] > size).astype(jnp.int32) for size in sizes[:-1])
    return lax.switch(choice, [with_tiles(i, size) for i, size in enumerate(sizes)])


def solution(mesh):
    in_specs = (
        P(("ctx", "head"), None),
        P(("ctx", "head"), None),
        P("ctx", None),
        P(),
        P(),
        P(),
        P(),
        P(),
    )
    out_specs = P("head", None, "ctx", None)
    return jax.shard_map(body, mesh=mesh, in_specs=in_specs, out_specs=out_specs, check_vma=False)
```

```python
import functools
import math

import jax
import jax.numpy as jnp
from jax import lax
from jax.experimental import pallas as pl
from jax.experimental.pallas import tpu as pltpu
from jax.sharding import PartitionSpec as P

QUERY_HEADS = 28
KEY_VALUE_HEADS = 4
HEAD_SIZE = 128
BLOCK_TOKENS = 64
SPAN = 4
SLASH = 4
GROUP_WIDTH = QUERY_HEADS // KEY_VALUE_HEADS

masked_score = -1e30
INFO = 8
LEAD = SPAN * BLOCK_TOKENS
PAIR = 2 * BLOCK_TOKENS


def pick_kernel(
    owners,
    total_blocks,
    shard_blocks,
    capacity,
    list_length,
    vert_index_in,
    vert_count_in,
    slash_off_in,
    slash_count_in,
    head_owner_in,
    cache,
    picked,
    place,
    info,
    used,
    vert_index,
    vert_count,
    slash_off,
    slash_count,
    head_owner,
    seen,
    slots_of,
    tiles_of,
    sem,
    list_sems,
):
    me = lax.axis_index("head")
    shard = lax.axis_index("ctx")
    first = shard * shard_blocks
    lists = [
        pltpu.make_async_copy(src, dst, list_sems.at[i])
        for i, (src, dst) in enumerate(
            (
                (vert_index_in, vert_index),
                (vert_count_in, vert_count),
                (slash_off_in, slash_off),
                (slash_count_in, slash_count),
                (head_owner_in, head_owner),
            )
        )
    ]
    for copy in lists:
        copy.start()
    picked[...] = jnp.zeros_like(picked)
    unroll = 16
    table = owners * KEY_VALUE_HEADS * total_blocks

    @pl.loop(0, table // unroll)
    def _(i):
        for u in range(unroll):
            seen[i * unroll + u] = 0

    for o in range(owners):
        slots_of[o] = 0
        tiles_of[o] = 0
    for s in range(capacity + 1):
        for u in range(INFO):
            info[s * INFO + u] = shard if u == 5 else 0
        for j in range(list_length):
            place[s * list_length + j] = 0

    for copy in lists:
        copy.wait()

    def one_head(h, started):
        owner = head_owner[h]
        mine = owner == me
        rank = slots_of[owner]
        slots_of[owner] = rank + 1
        slot = jnp.where(mine, rank, capacity)
        group = h // GROUP_WIDTH
        count = vert_count[h]
        bits = 0
        for k in range(SLASH):
            bits = bits | jnp.where(k < slash_count[h], 1 << slash_off[h, k], 0)
        info[slot * INFO] = h
        info[slot * INFO + 1] = group
        info[slot * INFO + 2] = count
        info[slot * INFO + 3] = bits
        info[slot * INFO + 4] = 1
        base = (owner * KEY_VALUE_HEADS + group) * total_blocks

        def one_entry(j, carry):
            tiles, started = carry
            block = vert_index[h, j]
            old = seen[base + block]
            fresh = old == 0
            at = jnp.where(fresh, tiles, old - 1)
            seen[base + block] = at + 1
            place[slot * list_length + j] = at
            here = fresh & mine & (block >= first) & (block < first + shard_blocks)

            @pl.when(here)
            def _():
                row = pl.multiple_of((block - first) * BLOCK_TOKENS, BLOCK_TOKENS)
                column = pl.multiple_of(group * 2 * HEAD_SIZE, 2 * HEAD_SIZE)
                pltpu.make_async_copy(
                    cache.at[pl.ds(row, BLOCK_TOKENS), pl.ds(column, 2 * HEAD_SIZE)],
                    picked.at[at],
                    sem,
                ).start()

            return tiles + fresh.astype(jnp.int32), started + here.astype(jnp.int32)

        tiles, started = lax.fori_loop(0, count, one_entry, (tiles_of[owner], started))
        tiles_of[owner] = tiles
        return started

    started = lax.fori_loop(0, QUERY_HEADS, one_head, jnp.int32(0))
    most = tiles_of[0]
    for o in range(1, owners):
        most = jnp.maximum(most, tiles_of[o])
    used[0] = most

    @pl.loop(0, started)
    def _(i):
        pltpu.make_async_copy(
            cache.at[pl.ds(0, BLOCK_TOKENS), pl.ds(0, 2 * HEAD_SIZE)], picked.at[0], sem
        ).wait()


def attend_kernel(
    list_length, place, info, q_ref, kv_ref, tiles_ref, out_ref, lists, offset_of, sems
):
    s = pl.program_id(0)
    slots = pl.num_programs(0)
    listed = lists.at[s % 2]

    def fetch(slot):
        @pl.loop(0, info[slot * INFO + 2])
        def _(j):
            pltpu.make_async_copy(
                tiles_ref.at[place[slot * list_length + j]],
                lists.at[
                    slot % 2, pl.ds(pl.multiple_of(j * BLOCK_TOKENS, BLOCK_TOKENS), BLOCK_TOKENS)
                ],
                sems.at[slot % 2],
            ).start()

    scale = 1.0 / math.sqrt(HEAD_SIZE)
    count = info[s * INFO + 2]
    bits = info[s * INFO + 3]
    live = info[s * INFO + 4]
    rows = q_ref.shape[0]
    pairs = rows // PAIR
    window = LEAD + PAIR
    unlisted = 31
    contract = (((1,), (1,)), ((), ()))

    @pl.when(s == 0)
    def _():
        lists[...] = jnp.zeros_like(lists)
        fetch(0)
        row = lax.broadcasted_iota(jnp.int32, (PAIR, window), 0)
        column = lax.broadcasted_iota(jnp.int32, (PAIR, window), 1)
        offset = SPAN + row // BLOCK_TOKENS - column // BLOCK_TOKENS
        seen = (offset >= 0) & (offset < SPAN) & (column <= row + LEAD)
        for p in range(pairs):
            block = (info[5] * rows + p * PAIR + row) // BLOCK_TOKENS
            offset_of[p] = jnp.where(seen & (block >= offset), offset, unlisted)

    @pl.when(s + 1 < slots)
    def _():
        fetch(s + 1)

    @pl.loop(0, count)
    def _(j):
        pltpu.make_async_copy(
            tiles_ref.at[0], listed.at[pl.ds(0, BLOCK_TOKENS)], sems.at[s % 2]
        ).wait()

    @pl.when(live == 0)
    def _():
        out_ref[...] = jnp.zeros_like(out_ref)

    def attend_listed(length):
        width = length * BLOCK_TOKENS
        far = lax.dot_general(
            q_ref[...], lists[s % 2, :width, :HEAD_SIZE], contract, preferred_element_type=jnp.float32
        )
        spot = lax.broadcasted_iota(jnp.int32, (1, width), 1)
        far = jnp.where(spot < count * BLOCK_TOKENS, far, masked_score)
        near = []
        for p in range(pairs):
            scores = lax.dot_general(
                q_ref[p * PAIR : (p + 1) * PAIR, :],
                kv_ref[p * PAIR : p * PAIR + window, :HEAD_SIZE],
                contract,
                preferred_element_type=jnp.float32,
            )
            allowed = (lax.shift_right_logical(bits, offset_of[p]) & 1) != 0
            near.append(jnp.where(allowed, scores, masked_score))
        highest = jnp.maximum(
            jnp.max(far, axis=1, keepdims=True),
            jnp.concatenate([jnp.max(part, axis=1, keepdims=True) for part in near], axis=0),
        )
        far = jnp.exp((far - highest) * scale)
        total = jnp.sum(far, axis=1, keepdims=True)
        weighted = jnp.dot(
            far.astype(jnp.bfloat16),
            lists[s % 2, :width, HEAD_SIZE:],
            preferred_element_type=jnp.float32,
        )
        for p in range(pairs):
            part = slice(p * PAIR, (p + 1) * PAIR)
            weights = jnp.exp((near[p] - highest[part]) * scale)
            share_sum = total[part] + jnp.sum(weights, axis=1, keepdims=True)
            share = weighted[part] + jnp.dot(
                weights.astype(jnp.bfloat16),
                kv_ref[p * PAIR : p * PAIR + window, HEAD_SIZE:],
                preferred_element_type=jnp.float32,
            )
            out_ref[0, 0, part, :] = (share / share_sum).astype(jnp.bfloat16)

    step = max(list_length // 3, 1)
    for length in range(step, list_length + 1, step):

        @pl.when((live != 0) & (count > length - step) & (count <= length))
        def _():
            attend_listed(length)


def attend(place, info, queries, extended, tiles, capacity, list_length):
    rows = queries.shape[0]
    return pl.pallas_call(
        functools.partial(attend_kernel, list_length),
        out_shape=jax.ShapeDtypeStruct((1, capacity, rows, HEAD_SIZE), jnp.bfloat16),
        grid_spec=pltpu.PrefetchScalarGridSpec(
            num_scalar_prefetch=2,
            grid=(capacity,),
            in_specs=[
                pl.BlockSpec((rows, HEAD_SIZE), lambda s, place, info: (0, info[s * INFO])),
                pl.BlockSpec(
                    (extended.shape[0], 2 * HEAD_SIZE),
                    lambda s, place, info: (0, info[s * INFO + 1]),
                ),
                pl.BlockSpec(memory_space=pl.ANY),
            ],
            out_specs=pl.BlockSpec(
                (1, 1, rows, HEAD_SIZE), lambda s, place, info: (0, s, 0, 0)
            ),
            scratch_shapes=[
                pltpu.VMEM((2, list_length * BLOCK_TOKENS, 2 * HEAD_SIZE), jnp.bfloat16),
                pltpu.VMEM((rows // PAIR, PAIR, LEAD + PAIR), jnp.int32),
                pltpu.SemaphoreType.DMA((2,)),
            ],
        ),
        compiler_params=pltpu.CompilerParams(vmem_limit_bytes=48 * 1024 * 1024),
        name="attend",
    )(place, info, queries, extended, tiles)


CHUNK_TILES = 2
LAG = 3
MESH = pl.DeviceIdType.MESH


def share_kernel(
    size,
    chunk,
    picked,
    queries,
    local_kv,
    tiles,
    all_queries,
    extended,
    own,
    core_in,
    right_in,
    left_in,
    right_out,
    left_out,
    final,
    cross_in,
    done,
    zeros,
    core_sems,
    right_sems,
    left_sems,
    cross_sems,
    out_sems,
    local_sems,
    write_sems,
    query_sems,
    near_sems,
    behind_send,
    behind_recv,
):
    ctx = lax.axis_index("ctx")
    head = lax.axis_index("head")
    shards = lax.axis_size("ctx")
    core = ctx % 2
    x = (ctx // 2) % 2
    z = ctx // 4
    planes = shards // 4
    half = size // 2
    chunks = half // chunk
    other_core = (ctx + 1 - 2 * core, head)
    other_x = (ctx + 2 - 4 * x, head)
    up = (ctx + 4, head)
    down = (ctx - 4, head)
    other_head = (ctx, 1 - head)
    rows = queries.shape[0]
    has_up = z < planes - 1
    has_down = z > 0
    has_next = ctx < shards - 1
    has_previous = ctx > 0

    barrier = pltpu.get_barrier_semaphore()

    def greet(device):
        pl.semaphore_signal(barrier, inc=1, device_id=device, device_id_type=MESH)

    greet(other_core)
    greet(other_x)
    greet(other_head)

    @pl.when(has_up)
    def _():
        greet(up)

    @pl.when(has_down)
    def _():
        greet(down)

    @pl.when(has_next)
    def _():
        greet((ctx + 1, head))
        greet((ctx + 1, 1 - head))

    @pl.when(has_previous)
    def _():
        greet((ctx - 1, head))
        greet((ctx - 1, 1 - head))

    peers = 3 + jnp.where(has_up, 1, 0) + jnp.where(has_down, 1, 0)
    peers = peers + jnp.where(has_next, 2, 0) + jnp.where(has_previous, 2, 0)
    pl.semaphore_wait(barrier, peers)

    def remote(src, dst, send, recv, device):
        return pltpu.make_async_remote_copy(
            src_ref=src,
            dst_ref=dst,
            send_sem=send,
            recv_sem=recv,
            device_id=device,
            device_id_type=MESH,
        )

    def piece(base, k):
        return pl.ds(base + k * chunk, chunk)

    def own_copy(k):
        return pltpu.make_async_copy(
            picked.at[piece(core * half, k)], own.at[piece(0, k)], local_sems.at[k]
        )

    def core_copy(k):
        return remote(
            picked.at[piece((1 - core) * half, k)],
            core_in.at[piece(0, k)],
            core_sems.at[0, k],
            core_sems.at[1, k],
            other_core,
        )

    def right_copy(k):
        return remote(
            right_out.at[piece(0, k)],
            right_in.at[piece(0, k)],
            right_sems.at[0, k],
            right_sems.at[1, k],
            up,
        )

    def left_copy(k):
        return remote(
            left_out.at[piece(0, k)],
            left_in.at[piece(0, k)],
            left_sems.at[0, k],
            left_sems.at[1, k],
            down,
        )

    def cross_copy(k):
        return remote(
            final.at[piece(0, k)],
            cross_in.at[piece(0, k)],
            cross_sems.at[0, k],
            cross_sems.at[1, k],
            other_x,
        )

    def out_copy(k, base):
        return remote(
            done.at[piece(0, k)],
            tiles.at[piece(base, k)],
            out_sems.at[0, k],
            out_sems.at[1, k],
            other_core,
        )

    def write_copy(k):
        return pltpu.make_async_copy(
            done.at[piece(0, k)], tiles.at[piece(core * half, k)], write_sems.at[k]
        )

    @pl.loop(0, chunks)
    def _(k):
        own_copy(k).start()
        core_copy(k).start()

    mine = pl.ds(pl.multiple_of(head * rows, rows), rows)
    near = pl.ds(pl.multiple_of(LEAD + head * rows, BLOCK_TOKENS), rows)
    near_copy = remote(
        local_kv, extended.at[near], near_sems.at[0], near_sems.at[1], other_head
    )
    query_copy = remote(
        queries, all_queries.at[mine], query_sems.at[0], query_sems.at[1], other_head
    )
    near_here = pltpu.make_async_copy(local_kv, extended.at[near], near_sems.at[2])
    query_here = pltpu.make_async_copy(queries, all_queries.at[mine], query_sems.at[2])

    def behind_copy(which, target):
        src, dst = local_kv, extended.at[which * rows : (which + 1) * rows]
        device = (ctx + 1, head if target == 0 else 1 - head)
        return remote(src, dst, behind_send.at[target], behind_recv.at[which], device)

    zero_copy = pltpu.make_async_copy(zeros, extended.at[:LEAD], behind_recv.at[2])
    for which in range(2):

        @pl.when(has_next & (head == which))
        def _():
            behind_copy(which, 0).start()
            behind_copy(which, 1).start()

    near_copy.start()
    query_copy.start()
    near_here.start()
    query_here.start()

    @pl.when(jnp.logical_not(has_previous))
    def _():
        zeros[...] = jnp.zeros_like(zeros)
        zero_copy.start()

    @pl.when(jnp.logical_not(has_down))
    def _():
        right_in[...] = jnp.zeros_like(right_in)

    @pl.when(jnp.logical_not(has_up))
    def _():
        left_in[...] = jnp.zeros_like(left_in)

    late = LAG * jnp.maximum(z, planes - 1 - z)

    @pl.loop(0, chunks + LAG * planes)
    def _(t):
        @pl.when(t < chunks)
        def _():
            own_copy(t).wait()
            core_copy(t).wait_recv()
            at = piece(0, t)
            own[at] = own[at] + core_in[at]

        k_right = t - LAG * z

        @pl.when((k_right >= 0) & (k_right < chunks))
        def _():
            @pl.when(has_down)
            def _():
                right_copy(k_right).wait_recv()

            at = piece(0, k_right)
            right_out[at] = own[at] + right_in[at]

            @pl.when(has_up)
            def _():
                right_copy(k_right).start()

        k_left = t - LAG * (planes - 1 - z)

        @pl.when((k_left >= 0) & (k_left < chunks))
        def _():
            @pl.when(has_up)
            def _():
                left_copy(k_left).wait_recv()

            at = piece(0, k_left)
            left_out[at] = own[at] + left_in[at]

            @pl.when(has_down)
            def _():
                left_copy(k_left).start()

        k_cross = t - late

        @pl.when((k_cross >= 0) & (k_cross < chunks))
        def _():
            at = piece(0, k_cross)
            final[at] = right_out[at] + left_in[at]
            cross_copy(k_cross).start()

        k_done = k_cross - LAG

        @pl.when((k_done >= 0) & (k_done < chunks))
        def _():
            cross_copy(k_done).wait_recv()
            at = piece(0, k_done)
            done[at] = final[at] + cross_in[at]
            out_copy(k_done, core * half).start()
            write_copy(k_done).start()

    @pl.loop(0, chunks)
    def _(k):
        core_copy(k).wait_send()

        @pl.when(has_up)
        def _():
            right_copy(k).wait_send()

        @pl.when(has_down)
        def _():
            left_copy(k).wait_send()

        cross_copy(k).wait_send()
        out_copy(k, core * half).wait_send()
        out_copy(k, (1 - core) * half).wait_recv()
        write_copy(k).wait()

    near_copy.wait()
    query_copy.wait()
    near_here.wait()
    query_here.wait()
    for which in range(2):

        @pl.when(has_next & (head == which))
        def _():
            behind_copy(which, 0).wait_send()
            behind_copy(which, 1).wait_send()

        @pl.when(has_previous)
        def _():
            behind_copy(which, 0).wait_recv()

    @pl.when(jnp.logical_not(has_previous))
    def _():
        zero_copy.wait()


def share(picked, queries, local_key_value, size, number):
    chunk = CHUNK_TILES * (2 if size > 128 else 1)
    half = size // 2
    chunks = half // chunk
    rows, width = queries.shape
    kv_width = local_key_value.shape[1]
    tile = (BLOCK_TOKENS, 2 * HEAD_SIZE)
    hbm = pl.BlockSpec(memory_space=pl.ANY)
    pairs = pltpu.SemaphoreType.DMA((2, chunks))
    return pl.pallas_call(
        functools.partial(share_kernel, size, chunk),
        out_shape=(
            jax.ShapeDtypeStruct(picked.shape, jnp.bfloat16),
            jax.ShapeDtypeStruct((2 * rows, width), jnp.bfloat16),
            jax.ShapeDtypeStruct((LEAD + 2 * rows, kv_width), jnp.bfloat16),
        ),
        in_specs=[hbm] * 3,
        out_specs=(hbm,) * 3,
        scratch_shapes=[pltpu.VMEM((half,) + tile, jnp.bfloat16)] * 9
        + [pltpu.VMEM((LEAD, kv_width), jnp.bfloat16)]
        + [pairs] * 5
        + [pltpu.SemaphoreType.DMA((chunks,))] * 2
        + [pltpu.SemaphoreType.DMA((3,))] * 2
        + [pltpu.SemaphoreType.DMA((2,)), pltpu.SemaphoreType.DMA((3,))],
        compiler_params=pltpu.CompilerParams(
            collective_id=number, has_side_effects=True, vmem_limit_bytes=48 * 1024 * 1024
        ),
        name="share",
    )(picked, queries, local_key_value)


def body(
    queries,
    local_key_value,
    cached_key_value,
    vert_index,
    vert_count,
    slash_off,
    slash_count,
    head_owner,
):
    owners = lax.axis_size("head")
    shards = lax.axis_size("ctx")
    capacity = QUERY_HEADS // owners + 2
    list_length = vert_index.shape[1]
    shard_blocks = cached_key_value.shape[0] // BLOCK_TOKENS
    total_blocks = shard_blocks * shards
    most = capacity * list_length
    smem = pl.BlockSpec(memory_space=pltpu.SMEM)
    picked, place, info, used = pl.pallas_call(
        functools.partial(
            pick_kernel, owners, total_blocks, shard_blocks, capacity, list_length
        ),
        out_shape=(
            jax.ShapeDtypeStruct((most, BLOCK_TOKENS, 2 * HEAD_SIZE), jnp.bfloat16),
            jax.ShapeDtypeStruct(((capacity + 1) * list_length,), jnp.int32),
            jax.ShapeDtypeStruct(((capacity + 1) * INFO,), jnp.int32),
            jax.ShapeDtypeStruct((1,), jnp.int32),
        ),
        in_specs=[pl.BlockSpec(memory_space=pltpu.HBM)] * 6,
        out_specs=(pl.BlockSpec(memory_space=pltpu.VMEM), smem, smem, smem),
        scratch_shapes=[
            pltpu.SMEM(array.shape, jnp.int32)
            for array in (vert_index, vert_count, slash_off, slash_count, head_owner)
        ]
        + [
            pltpu.SMEM((owners * KEY_VALUE_HEADS * total_blocks,), jnp.int32),
            pltpu.SMEM((owners,), jnp.int32),
            pltpu.SMEM((owners,), jnp.int32),
            pltpu.SemaphoreType.DMA,
            pltpu.SemaphoreType.DMA((5,)),
        ],
        compiler_params=pltpu.CompilerParams(vmem_limit_bytes=32 * 1024 * 1024),
        name="pick",
    )(vert_index, vert_count, slash_off, slash_count, head_owner, cached_key_value)

    own_plan = owners == 2 and shards == 16 and queries.shape[0] == 2 * BLOCK_TOKENS

    def with_tiles(number, size):
        def run():
            if own_plan:
                return share(picked, queries, local_key_value, size, number)
            gathered = lax.all_gather(queries, "head", axis=0, tiled=True)
            near = lax.all_gather(local_key_value, "head", axis=0, tiled=True)
            route = [(i, i + 1) for i in range(shards - 1)]
            behind = lax.ppermute(near[near.shape[0] - LEAD :], "ctx", route)
            extended = jnp.concatenate([behind, near], axis=0)
            tiles = lax.psum(picked[:size], "ctx")
            rest = jnp.zeros((most - size,) + tiles.shape[1:], tiles.dtype)
            return jnp.concatenate([tiles, rest], axis=0), gathered, extended

        return run

    sizes = [most * part // 24 for part in (9, 10, 11, 12, 14, 24)]
    choice = sum((used[0] > size).astype(jnp.int32) for size in sizes[:-1])
    tiles, gathered, extended = lax.switch(
        choice, [with_tiles(i, size) for i, size in enumerate(sizes)]
    )
    return attend(place, info, gathered, extended, tiles, capacity, list_length)


def solution(mesh):
    in_specs = (
        P(("ctx", "head"), None),
        P(("ctx", "head"), None),
        P("ctx", None),
        P(),
        P(),
        P(),
        P(),
        P(),
    )
    out_specs = P("head", None, "ctx", None)
    return jax.shard_map(body, mesh=mesh, in_specs=in_specs, out_specs=out_specs, check_vma=False)
```

```python
import functools
import math

import jax
import jax.numpy as jnp
from jax import lax
from jax.experimental import pallas as pl
from jax.experimental.pallas import tpu as pltpu
from jax.sharding import PartitionSpec as P

QUERY_HEADS = 28
KEY_VALUE_HEADS = 4
HEAD_SIZE = 128
BLOCK_TOKENS = 64
SPAN = 4
SLASH = 4
GROUP_WIDTH = QUERY_HEADS // KEY_VALUE_HEADS

masked_score = -1e30
INFO = 8
WRITE_TILES = 8
LEAD = SPAN * BLOCK_TOKENS
PAIR = 2 * BLOCK_TOKENS


def pick_kernel(
    owners,
    total_blocks,
    shard_blocks,
    capacity,
    list_length,
    vert_index_in,
    vert_count_in,
    slash_off_in,
    slash_count_in,
    head_owner_in,
    cache,
    picked_out,
    place,
    info,
    used,
    picked,
    vert_index,
    vert_count,
    slash_off,
    slash_count,
    head_owner,
    seen,
    slots_of,
    tiles_of,
    sem,
    list_sems,
    out_sem,
):
    me = lax.axis_index("head")
    shard = lax.axis_index("ctx")
    first = shard * shard_blocks
    lists = [
        pltpu.make_async_copy(src, dst, list_sems.at[i])
        for i, (src, dst) in enumerate(
            (
                (vert_index_in, vert_index),
                (vert_count_in, vert_count),
                (slash_off_in, slash_off),
                (slash_count_in, slash_count),
                (head_owner_in, head_owner),
            )
        )
    ]
    for copy in lists:
        copy.start()
    picked[...] = jnp.zeros_like(picked)
    unroll = 16
    table = owners * KEY_VALUE_HEADS * total_blocks

    @pl.loop(0, table // unroll)
    def _(i):
        for u in range(unroll):
            seen[i * unroll + u] = 0

    for o in range(owners):
        slots_of[o] = 0
        tiles_of[o] = 0
    for s in range(capacity + 1):
        for u in range(INFO):
            info[s * INFO + u] = shard if u == 5 else 0
        for j in range(list_length):
            place[s * list_length + j] = 0

    for copy in lists:
        copy.wait()

    def one_head(h, started):
        owner = head_owner[h]
        mine = owner == me
        rank = slots_of[owner]
        slots_of[owner] = rank + 1
        slot = jnp.where(mine, rank, capacity)
        group = h // GROUP_WIDTH
        count = vert_count[h]
        bits = 0
        for k in range(SLASH):
            bits = bits | jnp.where(k < slash_count[h], 1 << slash_off[h, k], 0)
        info[slot * INFO] = h
        info[slot * INFO + 1] = group
        info[slot * INFO + 2] = count
        info[slot * INFO + 3] = bits
        info[slot * INFO + 4] = 1
        base = (owner * KEY_VALUE_HEADS + group) * total_blocks

        def one_entry(j, carry):
            tiles, started = carry
            block = vert_index[h, j]
            old = seen[base + block]
            fresh = old == 0
            at = jnp.where(fresh, tiles, old - 1)
            seen[base + block] = at + 1
            place[slot * list_length + j] = at
            here = fresh & mine & (block >= first) & (block < first + shard_blocks)

            @pl.when(here)
            def _():
                row = pl.multiple_of((block - first) * BLOCK_TOKENS, BLOCK_TOKENS)
                column = pl.multiple_of(group * 2 * HEAD_SIZE, 2 * HEAD_SIZE)
                pltpu.make_async_copy(
                    cache.at[pl.ds(row, BLOCK_TOKENS), pl.ds(column, 2 * HEAD_SIZE)],
                    picked.at[at],
                    sem,
                ).start()

            return tiles + fresh.astype(jnp.int32), started + here.astype(jnp.int32)

        tiles, started = lax.fori_loop(0, count, one_entry, (tiles_of[owner], started))
        tiles_of[owner] = tiles
        return started

    started = lax.fori_loop(0, QUERY_HEADS, one_head, jnp.int32(0))
    most = tiles_of[0]
    for o in range(1, owners):
        most = jnp.maximum(most, tiles_of[o])
    used[0] = most

    @pl.loop(0, started)
    def _(i):
        pltpu.make_async_copy(
            cache.at[pl.ds(0, BLOCK_TOKENS), pl.ds(0, 2 * HEAD_SIZE)], picked.at[0], sem
        ).wait()

    def write_out(i):
        piece = pl.ds(i * WRITE_TILES, WRITE_TILES)
        return pltpu.make_async_copy(picked.at[piece], picked_out.at[piece], out_sem)

    pieces = (most + WRITE_TILES - 1) // WRITE_TILES

    @pl.loop(0, pieces)
    def _(i):
        write_out(i).start()

    @pl.loop(0, pieces)
    def _(i):
        write_out(i).wait()


def attend_kernel(
    list_length, place, info, q_ref, kv_ref, tiles_ref, out_ref, lists, offset_of, sems
):
    s = pl.program_id(0)
    slots = pl.num_programs(0)
    listed = lists.at[s % 2]

    def fetch(slot):
        @pl.loop(0, info[slot * INFO + 2])
        def _(j):
            pltpu.make_async_copy(
                tiles_ref.at[place[slot * list_length + j]],
                lists.at[
                    slot % 2, pl.ds(pl.multiple_of(j * BLOCK_TOKENS, BLOCK_TOKENS), BLOCK_TOKENS)
                ],
                sems.at[slot % 2],
            ).start()

    scale = 1.0 / math.sqrt(HEAD_SIZE)
    count = info[s * INFO + 2]
    bits = info[s * INFO + 3]
    live = info[s * INFO + 4]
    rows = q_ref.shape[0]
    pairs = rows // PAIR
    window = LEAD + PAIR
    unlisted = 31
    contract = (((1,), (1,)), ((), ()))

    @pl.when(s == 0)
    def _():
        lists[...] = jnp.zeros_like(lists)
        fetch(0)
        row = lax.broadcasted_iota(jnp.int32, (PAIR, window), 0)
        column = lax.broadcasted_iota(jnp.int32, (PAIR, window), 1)
        offset = SPAN + row // BLOCK_TOKENS - column // BLOCK_TOKENS
        seen = (offset >= 0) & (offset < SPAN) & (column <= row + LEAD)
        for p in range(pairs):
            block = (info[5] * rows + p * PAIR + row) // BLOCK_TOKENS
            offset_of[p] = jnp.where(seen & (block >= offset), offset, unlisted)

    @pl.when(s + 1 < slots)
    def _():
        fetch(s + 1)

    @pl.loop(0, count)
    def _(j):
        pltpu.make_async_copy(
            tiles_ref.at[0], listed.at[pl.ds(0, BLOCK_TOKENS)], sems.at[s % 2]
        ).wait()

    @pl.when(live == 0)
    def _():
        out_ref[...] = jnp.zeros_like(out_ref)

    def attend_listed(length):
        width = length * BLOCK_TOKENS
        far = lax.dot_general(
            q_ref[...], lists[s % 2, :width, :HEAD_SIZE], contract, preferred_element_type=jnp.float32
        )
        spot = lax.broadcasted_iota(jnp.int32, (1, width), 1)
        far = jnp.where(spot < count * BLOCK_TOKENS, far, masked_score)
        near = []
        for p in range(pairs):
            scores = lax.dot_general(
                q_ref[p * PAIR : (p + 1) * PAIR, :],
                kv_ref[p * PAIR : p * PAIR + window, :HEAD_SIZE],
                contract,
                preferred_element_type=jnp.float32,
            )
            allowed = (lax.shift_right_logical(bits, offset_of[p]) & 1) != 0
            near.append(jnp.where(allowed, scores, masked_score))
        highest = jnp.maximum(
            jnp.max(far, axis=1, keepdims=True),
            jnp.concatenate([jnp.max(part, axis=1, keepdims=True) for part in near], axis=0),
        )
        far = jnp.exp((far - highest) * scale)
        total = jnp.sum(far, axis=1, keepdims=True)
        weighted = jnp.dot(
            far.astype(jnp.bfloat16),
            lists[s % 2, :width, HEAD_SIZE:],
            preferred_element_type=jnp.float32,
        )
        for p in range(pairs):
            part = slice(p * PAIR, (p + 1) * PAIR)
            weights = jnp.exp((near[p] - highest[part]) * scale)
            share_sum = total[part] + jnp.sum(weights, axis=1, keepdims=True)
            share = weighted[part] + jnp.dot(
                weights.astype(jnp.bfloat16),
                kv_ref[p * PAIR : p * PAIR + window, HEAD_SIZE:],
                preferred_element_type=jnp.float32,
            )
            out_ref[0, 0, part, :] = (share / share_sum).astype(jnp.bfloat16)

    step = max(list_length // 3, 1)
    for length in range(step, list_length + 1, step):

        @pl.when((live != 0) & (count > length - step) & (count <= length))
        def _():
            attend_listed(length)


def attend(place, info, queries, extended, tiles, capacity, list_length):
    rows = queries.shape[0]
    return pl.pallas_call(
        functools.partial(attend_kernel, list_length),
        out_shape=jax.ShapeDtypeStruct((1, capacity, rows, HEAD_SIZE), jnp.bfloat16),
        grid_spec=pltpu.PrefetchScalarGridSpec(
            num_scalar_prefetch=2,
            grid=(capacity,),
            in_specs=[
                pl.BlockSpec((rows, HEAD_SIZE), lambda s, place, info: (0, info[s * INFO])),
                pl.BlockSpec(
                    (extended.shape[0], 2 * HEAD_SIZE),
                    lambda s, place, info: (0, info[s * INFO + 1]),
                ),
                pl.BlockSpec(memory_space=pl.ANY),
            ],
            out_specs=pl.BlockSpec(
                (1, 1, rows, HEAD_SIZE), lambda s, place, info: (0, s, 0, 0)
            ),
            scratch_shapes=[
                pltpu.VMEM((2, list_length * BLOCK_TOKENS, 2 * HEAD_SIZE), jnp.bfloat16),
                pltpu.VMEM((rows // PAIR, PAIR, LEAD + PAIR), jnp.int32),
                pltpu.SemaphoreType.DMA((2,)),
            ],
        ),
        compiler_params=pltpu.CompilerParams(vmem_limit_bytes=48 * 1024 * 1024),
        name="attend",
    )(place, info, queries, extended, tiles)


CHUNK_TILES = 2
LAG = 3
MESH = pl.DeviceIdType.MESH


def share_kernel(
    size,
    chunk,
    picked,
    queries,
    local_kv,
    tiles,
    all_queries,
    extended,
    own,
    core_in,
    right_in,
    left_in,
    right_out,
    left_out,
    final,
    cross_in,
    done,
    zeros,
    core_sems,
    right_sems,
    left_sems,
    cross_sems,
    out_sems,
    local_sems,
    write_sems,
    query_sems,
    near_sems,
    behind_send,
    behind_recv,
):
    ctx = lax.axis_index("ctx")
    head = lax.axis_index("head")
    shards = lax.axis_size("ctx")
    core = ctx % 2
    x = (ctx // 2) % 2
    z = ctx // 4
    planes = shards // 4
    half = size // 2
    chunks = half // chunk
    other_core = (ctx + 1 - 2 * core, head)
    other_x = (ctx + 2 - 4 * x, head)
    up = (ctx + 4, head)
    down = (ctx - 4, head)
    other_head = (ctx, 1 - head)
    rows = queries.shape[0]
    has_up = z < planes - 1
    has_down = z > 0
    has_next = ctx < shards - 1
    has_previous = ctx > 0

    barrier = pltpu.get_barrier_semaphore()

    def greet(device):
        pl.semaphore_signal(barrier, inc=1, device_id=device, device_id_type=MESH)

    greet(other_core)
    greet(other_x)
    greet(other_head)

    @pl.when(has_up)
    def _():
        greet(up)

    @pl.when(has_down)
    def _():
        greet(down)

    @pl.when(has_next)
    def _():
        greet((ctx + 1, head))
        greet((ctx + 1, 1 - head))

    @pl.when(has_previous)
    def _():
        greet((ctx - 1, head))
        greet((ctx - 1, 1 - head))

    peers = 3 + jnp.where(has_up, 1, 0) + jnp.where(has_down, 1, 0)
    peers = peers + jnp.where(has_next, 2, 0) + jnp.where(has_previous, 2, 0)
    pl.semaphore_wait(barrier, peers)

    def remote(src, dst, send, recv, device):
        return pltpu.make_async_remote_copy(
            src_ref=src,
            dst_ref=dst,
            send_sem=send,
            recv_sem=recv,
            device_id=device,
            device_id_type=MESH,
        )

    def piece(base, k):
        return pl.ds(base + k * chunk, chunk)

    def own_copy(k):
        return pltpu.make_async_copy(
            picked.at[piece(core * half, k)], own.at[piece(0, k)], local_sems.at[k]
        )

    def core_copy(k):
        return remote(
            picked.at[piece((1 - core) * half, k)],
            core_in.at[piece(0, k)],
            core_sems.at[0, k],
            core_sems.at[1, k],
            other_core,
        )

    def right_copy(k):
        return remote(
            right_out.at[piece(0, k)],
            right_in.at[piece(0, k)],
            right_sems.at[0, k],
            right_sems.at[1, k],
            up,
        )

    def left_copy(k):
        return remote(
            left_out.at[piece(0, k)],
            left_in.at[piece(0, k)],
            left_sems.at[0, k],
            left_sems.at[1, k],
            down,
        )

    def cross_copy(k):
        return remote(
            final.at[piece(0, k)],
            cross_in.at[piece(0, k)],
            cross_sems.at[0, k],
            cross_sems.at[1, k],
            other_x,
        )

    def out_copy(k, base):
        return remote(
            done.at[piece(0, k)],
            tiles.at[piece(base, k)],
            out_sems.at[0, k],
            out_sems.at[1, k],
            other_core,
        )

    def write_copy(k):
        return pltpu.make_async_copy(
            done.at[piece(0, k)], tiles.at[piece(core * half, k)], write_sems.at[k]
        )

    @pl.loop(0, chunks)
    def _(k):
        own_copy(k).start()
        core_copy(k).start()

    mine = pl.ds(pl.multiple_of(head * rows, rows), rows)
    near = pl.ds(pl.multiple_of(LEAD + head * rows, BLOCK_TOKENS), rows)
    near_copy = remote(
        local_kv, extended.at[near], near_sems.at[0], near_sems.at[1], other_head
    )
    query_copy = remote(
        queries, all_queries.at[mine], query_sems.at[0], query_sems.at[1], other_head
    )
    near_here = pltpu.make_async_copy(local_kv, extended.at[near], near_sems.at[2])
    query_here = pltpu.make_async_copy(queries, all_queries.at[mine], query_sems.at[2])

    def behind_copy(which, target):
        src, dst = local_kv, extended.at[which * rows : (which + 1) * rows]
        device = (ctx + 1, head if target == 0 else 1 - head)
        return remote(src, dst, behind_send.at[target], behind_recv.at[which], device)

    zero_copy = pltpu.make_async_copy(zeros, extended.at[:LEAD], behind_recv.at[2])
    for which in range(2):

        @pl.when(has_next & (head == which))
        def _():
            behind_copy(which, 0).start()
            behind_copy(which, 1).start()

    near_copy.start()
    query_copy.start()
    near_here.start()
    query_here.start()

    @pl.when(jnp.logical_not(has_previous))
    def _():
        zeros[...] = jnp.zeros_like(zeros)
        zero_copy.start()

    @pl.when(jnp.logical_not(has_down))
    def _():
        right_in[...] = jnp.zeros_like(right_in)

    @pl.when(jnp.logical_not(has_up))
    def _():
        left_in[...] = jnp.zeros_like(left_in)

    late = LAG * jnp.maximum(z, planes - 1 - z)

    @pl.loop(0, chunks + LAG * planes)
    def _(t):
        @pl.when(t < chunks)
        def _():
            own_copy(t).wait()
            core_copy(t).wait_recv()
            at = piece(0, t)
            own[at] = own[at] + core_in[at]

        k_right = t - LAG * z

        @pl.when((k_right >= 0) & (k_right < chunks))
        def _():
            @pl.when(has_down)
            def _():
                right_copy(k_right).wait_recv()

            at = piece(0, k_right)
            right_out[at] = own[at] + right_in[at]

            @pl.when(has_up)
            def _():
                right_copy(k_right).start()

        k_left = t - LAG * (planes - 1 - z)

        @pl.when((k_left >= 0) & (k_left < chunks))
        def _():
            @pl.when(has_up)
            def _():
                left_copy(k_left).wait_recv()

            at = piece(0, k_left)
            left_out[at] = own[at] + left_in[at]

            @pl.when(has_down)
            def _():
                left_copy(k_left).start()

        k_cross = t - late

        @pl.when((k_cross >= 0) & (k_cross < chunks))
        def _():
            at = piece(0, k_cross)
            final[at] = right_out[at] + left_in[at]
            cross_copy(k_cross).start()

        k_done = k_cross - LAG

        @pl.when((k_done >= 0) & (k_done < chunks))
        def _():
            cross_copy(k_done).wait_recv()
            at = piece(0, k_done)
            done[at] = final[at] + cross_in[at]
            out_copy(k_done, core * half).start()
            write_copy(k_done).start()

    @pl.loop(0, chunks)
    def _(k):
        core_copy(k).wait_send()

        @pl.when(has_up)
        def _():
            right_copy(k).wait_send()

        @pl.when(has_down)
        def _():
            left_copy(k).wait_send()

        cross_copy(k).wait_send()
        out_copy(k, core * half).wait_send()
        out_copy(k, (1 - core) * half).wait_recv()
        write_copy(k).wait()

    near_copy.wait()
    query_copy.wait()
    near_here.wait()
    query_here.wait()
    for which in range(2):

        @pl.when(has_next & (head == which))
        def _():
            behind_copy(which, 0).wait_send()
            behind_copy(which, 1).wait_send()

        @pl.when(has_previous)
        def _():
            behind_copy(which, 0).wait_recv()

    @pl.when(jnp.logical_not(has_previous))
    def _():
        zero_copy.wait()


def share(picked, queries, local_key_value, size, number):
    chunk = CHUNK_TILES * (2 if size > 128 else 1)
    half = size // 2
    chunks = half // chunk
    rows, width = queries.shape
    kv_width = local_key_value.shape[1]
    tile = (BLOCK_TOKENS, 2 * HEAD_SIZE)
    hbm = pl.BlockSpec(memory_space=pl.ANY)
    pairs = pltpu.SemaphoreType.DMA((2, chunks))
    return pl.pallas_call(
        functools.partial(share_kernel, size, chunk),
        out_shape=(
            jax.ShapeDtypeStruct(picked.shape, jnp.bfloat16),
            jax.ShapeDtypeStruct((2 * rows, width), jnp.bfloat16),
            jax.ShapeDtypeStruct((LEAD + 2 * rows, kv_width), jnp.bfloat16),
        ),
        in_specs=[hbm] * 3,
        out_specs=(hbm,) * 3,
        scratch_shapes=[pltpu.VMEM((half,) + tile, jnp.bfloat16)] * 9
        + [pltpu.VMEM((LEAD, kv_width), jnp.bfloat16)]
        + [pairs] * 5
        + [pltpu.SemaphoreType.DMA((chunks,))] * 2
        + [pltpu.SemaphoreType.DMA((3,))] * 2
        + [pltpu.SemaphoreType.DMA((2,)), pltpu.SemaphoreType.DMA((3,))],
        compiler_params=pltpu.CompilerParams(
            collective_id=number, has_side_effects=True, vmem_limit_bytes=48 * 1024 * 1024
        ),
        name="share",
    )(picked, queries, local_key_value)


def body(
    queries,
    local_key_value,
    cached_key_value,
    vert_index,
    vert_count,
    slash_off,
    slash_count,
    head_owner,
):
    owners = lax.axis_size("head")
    shards = lax.axis_size("ctx")
    capacity = QUERY_HEADS // owners + 2
    list_length = vert_index.shape[1]
    shard_blocks = cached_key_value.shape[0] // BLOCK_TOKENS
    total_blocks = shard_blocks * shards
    most = capacity * list_length
    smem = pl.BlockSpec(memory_space=pltpu.SMEM)
    picked, place, info, used = pl.pallas_call(
        functools.partial(
            pick_kernel, owners, total_blocks, shard_blocks, capacity, list_length
        ),
        out_shape=(
            jax.ShapeDtypeStruct((most, BLOCK_TOKENS, 2 * HEAD_SIZE), jnp.bfloat16),
            jax.ShapeDtypeStruct(((capacity + 1) * list_length,), jnp.int32),
            jax.ShapeDtypeStruct(((capacity + 1) * INFO,), jnp.int32),
            jax.ShapeDtypeStruct((1,), jnp.int32),
        ),
        in_specs=[pl.BlockSpec(memory_space=pltpu.HBM)] * 6,
        out_specs=(pl.BlockSpec(memory_space=pl.ANY), smem, smem, smem),
        scratch_shapes=[pltpu.VMEM((most, BLOCK_TOKENS, 2 * HEAD_SIZE), jnp.bfloat16)]
        + [
            pltpu.SMEM(array.shape, jnp.int32)
            for array in (vert_index, vert_count, slash_off, slash_count, head_owner)
        ]
        + [
            pltpu.SMEM((owners * KEY_VALUE_HEADS * total_blocks,), jnp.int32),
            pltpu.SMEM((owners,), jnp.int32),
            pltpu.SMEM((owners,), jnp.int32),
            pltpu.SemaphoreType.DMA,
            pltpu.SemaphoreType.DMA((5,)),
            pltpu.SemaphoreType.DMA,
        ],
        compiler_params=pltpu.CompilerParams(vmem_limit_bytes=60 * 1024 * 1024),
        name="pick",
    )(vert_index, vert_count, slash_off, slash_count, head_owner, cached_key_value)

    own_plan = owners == 2 and shards == 16 and queries.shape[0] == 2 * BLOCK_TOKENS

    def with_tiles(number, size):
        def run():
            if own_plan:
                return share(picked, queries, local_key_value, size, number)
            gathered = lax.all_gather(queries, "head", axis=0, tiled=True)
            near = lax.all_gather(local_key_value, "head", axis=0, tiled=True)
            route = [(i, i + 1) for i in range(shards - 1)]
            behind = lax.ppermute(near[near.shape[0] - LEAD :], "ctx", route)
            extended = jnp.concatenate([behind, near], axis=0)
            tiles = lax.psum(picked[:size], "ctx")
            rest = jnp.zeros((most - size,) + tiles.shape[1:], tiles.dtype)
            return jnp.concatenate([tiles, rest], axis=0), gathered, extended

        return run

    sizes = [most * part // 24 for part in (9, 10, 11, 12, 14, 24)]
    choice = sum((used[0] > size).astype(jnp.int32) for size in sizes[:-1])
    tiles, gathered, extended = lax.switch(
        choice, [with_tiles(i, size) for i, size in enumerate(sizes)]
    )
    return attend(place, info, gathered, extended, tiles, capacity, list_length)


def solution(mesh):
    in_specs = (
        P(("ctx", "head"), None),
        P(("ctx", "head"), None),
        P("ctx", None),
        P(),
        P(),
        P(),
        P(),
        P(),
    )
    out_specs = P("head", None, "ctx", None)
    return jax.shard_map(body, mesh=mesh, in_specs=in_specs, out_specs=out_specs, check_vma=False)
```
